768 devices in a mesh: seq: 48 (over y, z_hi, core), col: 16 (over x, z_lo).
Axes of the slice: x: 4, y: 8, z: 12 (z_hi: 3, z_lo: 4; z = z_hi * 4 + z_lo), core: 2. Of those that a mesh axis runs over, the one named last changes fastest.
Arguments:
- outer_gate: bfloat16 [3072, 12288], P('col', 'seq'), may hold values from -6 to 6
- inner_gate: bfloat16 [3072, 12288], P('col', 'seq'), may hold values from -6 to 6
- value_proj: bfloat16 [3072, 12288], P('col', 'seq'), may hold values from -6 to 6
- residues: float32 [3072, 16], P('col'), may hold values from -1.5 to 1.5
- decays: float32 [3072, 16], P('col'), may hold values from 2.4414062e-05 to 0.04
- out_weight: bfloat16 [3072, 4096], P(None, 'col'), may hold values from -0.15625 to 0.15625
- out_grad: bfloat16 [12288, 4096], P('seq', 'col'), may hold values from -6 to 6
Outputs:
- mixed: bfloat16 [12288, 4096], P('seq', 'col')
- grad_outer: bfloat16 [3072, 12288], P('col', 'seq')
- grad_inner: bfloat16 [3072, 12288], P('col', 'seq')
- grad_value: bfloat16 [3072, 12288], P('col', 'seq')
- grad_weight: float32 [3072, 4096], P('seq', 'col')
The draws below stay inside these ranges and needn't reach their ends.
All inputs are finite; a program needn't handle non-finite values.
Results may differ from the reference program's by a relative error of at most 0.0064.
Values may be sent and summed in bfloat16 or wider, within the bound.
No kernel may reach another device: no remote copies, remote signals or barrier semaphores. Data moves between devices by JAX's collectives and lax.ppermute only.
A program may use at most 64 MiB of HBM per device.

```python
import math
import jax
import jax.numpy as jnp

D = 4096
C = 3072
K = 16
TOKENS = 12288


def draw_decays(key, part):
    key = jax.random.fold_in(key, 7)
    first, second, third = jax.random.split(key, 3)
    slow_low = math.log(0.3 / TOKENS)
    slow_high = math.log(2.3 / TOKENS)
    fast_high = math.log(0.04)
    share = 0.5
    slow = jnp.exp(jax.random.uniform(first, (C, K), jnp.float32, slow_low, slow_high))
    fast = jnp.exp(jax.random.uniform(second, (C, K), jnp.float32, slow_high, fast_high))
    picked = jax.random.uniform(third, (C, K), jnp.float32) < share
    return jnp.where(picked, slow, fast).astype(jnp.float32)


def raised(entries, own_key, source, target, blocks, factor):
    owner, partner = [(jnp.arange(entries.shape[axis_at]) // (entries.shape[axis_at] // blocks)).reshape([-1 if axis == axis_at else 1 for axis in range(entries.ndim)]) for axis_at in (source, target)]
    chosen = jax.random.permutation(own_key, blocks)[partner]
    strong = (owner == chosen) | (owner == (partner + blocks // 2) % blocks)
    return jnp.where(strong, factor * entries, entries)


def steps_of(stream_key, extent, shards, smallest, top_value):
    gain = 1.0
    for position, shards_of in shards:
        draws = jax.random.uniform(jax.random.fold_in(jax.random.fold_in(stream_key, 6), position), (shards_of,), jnp.float32, smallest / len(shards), top_value / len(shards))
        gain = gain * jnp.repeat(jnp.exp(draws), extent[position] // shards_of).reshape((-1,) + (1,) * (len(extent) - 1 - position))
    return gain


def gaussian(rng, extent, scale, reach, shards=(), kind=jnp.bfloat16):
    entries = scale * jax.random.normal(rng, extent, jnp.float32)
    if shards:
        entries = entries * steps_of(rng, extent, shards, -0.22, 0.18)
    return jnp.clip(entries, -reach, reach).astype(kind)


def gaussian_with(stream_key, dims, scale, most, pieces, heavy, kind=jnp.bfloat16):
    drawn = scale * jax.random.normal(stream_key, dims, jnp.float32)
    if pieces:
        drawn = drawn * steps_of(stream_key, dims, pieces, -0.22, 0.18)
    return jnp.clip(raised(drawn, jax.random.fold_in(stream_key, 3), *heavy), -most, most).astype(kind)


def setup_inputs(seed: int = 0) -> dict:
    keys = jax.random.split(jax.random.key(seed), 8)
    return {
        "outer_gate": gaussian_with(keys[0], (C, TOKENS), 1.0, 6.0, ((0, 16), (1, 48)), (1, 0, 48, 3.25)),
        "inner_gate": gaussian(keys[1], (C, TOKENS), 1.0, 6.0, ((0, 16), (1, 48))),
        "value_proj": gaussian(keys[2], (C, TOKENS), 1.0, 6.0, ((0, 16), (1, 48))),
        "residues": gaussian(keys[3], (C, K), 0.25, 1.5, ((0, 16),), jnp.float32),
        "decays": draw_decays(jax.random.fold_in(keys[7], 71), 0),
        "out_weight": gaussian_with(keys[5], (C, D), C ** -0.5, 0.15625, ((1, 16),), (1, 0, 16, 2.0)),
        "out_grad": gaussian(keys[6], (TOKENS, D), 1.0, 6.0, ((0, 48), (1, 16))),
    }


def impulse_table(residues, decays):
    coef = residues * jnp.sqrt(-jnp.expm1(-2.0 * decays))
    times = jnp.arange(TOKENS, dtype=jnp.float32)
    table = jnp.zeros((residues.shape[0], TOKENS), jnp.float32)
    for mode in range(K):
        table = table + coef[:, mode:mode + 1] * jnp.exp(-decays[:, mode:mode + 1] * times[None, :])
    return table

def causal_filter(signal, spectrum):
    length = 2 * TOKENS
    result = jnp.fft.irfft(jnp.fft.rfft(signal, n=length, axis=1) * spectrum, n=length, axis=1)
    return result[:, :TOKENS].astype(signal.dtype)

def reference(outer_gate, inner_gate, value_proj, residues, decays, out_weight, out_grad):
    table = impulse_table(residues, decays)
    spectrum = jnp.fft.rfft(table, n=2 * TOKENS, axis=1)
    gated = (inner_gate.astype(jnp.float32) * value_proj.astype(jnp.float32)).astype(jnp.bfloat16)
    filtered = causal_filter(gated.astype(jnp.float32), spectrum).astype(jnp.bfloat16)
    product = (outer_gate.astype(jnp.float32) * filtered.astype(jnp.float32)).astype(jnp.bfloat16)
    mixed = jnp.dot(product.T, out_weight, preferred_element_type=jnp.float32).astype(jnp.bfloat16)
    back_sum = jnp.dot(out_weight, out_grad.T, preferred_element_type=jnp.float32)
    grad_outer = (back_sum * filtered.astype(jnp.float32)).astype(jnp.bfloat16)
    back_filtered = (back_sum * outer_gate.astype(jnp.float32)).astype(jnp.bfloat16)
    flipped = jnp.flip(back_filtered.astype(jnp.float32), 1)
    back_gated = jnp.flip(causal_filter(flipped, spectrum), 1).astype(jnp.bfloat16)
    grad_inner = (back_gated.astype(jnp.float32) * value_proj.astype(jnp.float32)).astype(jnp.bfloat16)
    grad_value = (back_gated.astype(jnp.float32) * inner_gate.astype(jnp.float32)).astype(jnp.bfloat16)
    grad_weight = jnp.dot(product, out_grad, preferred_element_type=jnp.float32) * TOKENS ** (-0.5)
    return (mixed, grad_outer, grad_inner, grad_value, grad_weight)
```

```python
import math

import jax
import jax.numpy as jnp
from jax import lax
from jax.experimental import pallas as pl
from jax.experimental.pallas import tpu as pltpu
from jax.sharding import Mesh
from jax.sharding import PartitionSpec as P

f32 = jnp.float32
bf16 = jnp.bfloat16
SUB = 32
LANES = 128


def to_columns(tile):
    rows, width = tile.shape
    pad = jnp.zeros((LANES - rows, width), f32)
    return jnp.concatenate([tile, pad], axis=0).T


def scan_kernel(g_ref, r_ref, o_ref, d_ref, c_ref, yf_ref, yb_ref, bs_ref, sf_ref, sb_ref, gt, bt):
    width = g_ref.shape[2]
    for half in range(2):
        at = pl.ds(half * width, width)
        gt[at, :] = to_columns(g_ref[half].astype(f32))
        total = r_ref[0, :, at].astype(f32)
        for i in range(1, r_ref.shape[0]):
            total = total + r_ref[i, :, at].astype(f32)
        bs_ref[half] = total
        bt[at, :] = to_columns((total * o_ref[half].astype(f32)).astype(bf16).astype(f32))
    rate = jnp.exp(-d_ref[...])
    coef = c_ref[...]
    length = gt.shape[0]

    def step(i, carry):
        sf, sb = carry
        lo = pl.multiple_of(i * 8, 8)
        hi = pl.multiple_of(length - 8 - i * 8, 8)
        gs, bs = gt[pl.ds(lo, 8), :], bt[pl.ds(hi, 8), :]
        fs, rs = [], [None] * 8
        for t in range(8):
            sf = sf * rate + gs[t : t + 1, :]
            sb = sb * rate + bs[7 - t : 8 - t, :]
            fs.append(jnp.sum(sf * coef, axis=0, keepdims=True))
            rs[7 - t] = jnp.sum(sb * coef, axis=0, keepdims=True)
        yf_ref[pl.ds(lo, 8), :] = jnp.concatenate(fs, axis=0)
        yb_ref[pl.ds(hi, 8), :] = jnp.concatenate(rs, axis=0)
        return sf, sb

    zero = jnp.zeros_like(coef)
    sf, sb = lax.fori_loop(0, length // 8, step, (zero, zero))
    sf_ref[...] = sf
    sb_ref[...] = sb


def heads_kernel(me_ref, s_ref, d_ref, c_ref, yf_ref, yb_ref, o_ref, bs_ref, p_ref, go_ref, bg_ref, ft, bt):
    me = me_ref[0]
    decay = d_ref[...]
    rate = jnp.exp(-decay)
    coef = c_ref[...]
    length = ft.shape[0]
    chips = s_ref.shape[0]
    width = o_ref.shape[2]
    jump = jnp.exp(-decay * float(length))
    pf = jnp.zeros_like(coef)
    pb = jnp.zeros_like(coef)
    for m in range(chips):
        pf = jnp.where(m < me, pf * jump + s_ref[m], pf)
        back = chips - 1 - m
        pb = jnp.where(back > me, pb * jump + s_ref[back], pb)
    pf = pf * coef
    pb = pb * coef

    def step(i, carry):
        pf, pb = carry
        lo = pl.multiple_of(i * 8, 8)
        hi = pl.multiple_of(length - 8 - i * 8, 8)
        fs, rs = [], [None] * 8
        for t in range(8):
            pf = pf * rate
            pb = pb * rate
            fs.append(jnp.sum(pf, axis=0, keepdims=True))
            rs[7 - t] = jnp.sum(pb, axis=0, keepdims=True)
        ft[pl.ds(lo, 8), :] = yf_ref[pl.ds(lo, 8), :] + jnp.concatenate(fs, axis=0)
        bt[pl.ds(hi, 8), :] = yb_ref[pl.ds(hi, 8), :] + jnp.concatenate(rs, axis=0)
        return pf, pb

    lax.fori_loop(0, length // 8, step, (pf, pb))
    rows = o_ref.shape[1]
    for half in range(2):
        at = pl.ds(half * width, width)
        filtered = ft[at, :].T[:rows].astype(bf16).astype(f32)
        p_ref[:, at] = (o_ref[half].astype(f32) * filtered).astype(bf16)
        go_ref[half] = (bs_ref[half] * filtered).astype(bf16)
        bg_ref[half] = bt[at, :].T[:rows].astype(bf16)


def vmem(count):
    return [pl.BlockSpec(memory_space=pltpu.VMEM)] * count


params = pltpu.CompilerParams(vmem_limit_bytes=32 * 2**20)


def scan_call(gated, parts, outer, decay, coef):
    _, rows, width = gated.shape
    length = 2 * width
    modes = decay.shape[0]
    return pl.pallas_call(
        scan_kernel,
        out_shape=(
            jax.ShapeDtypeStruct((length, LANES), f32),
            jax.ShapeDtypeStruct((length, LANES), f32),
            jax.ShapeDtypeStruct((2, rows, width), f32),
            jax.ShapeDtypeStruct((modes, LANES), f32),
            jax.ShapeDtypeStruct((modes, LANES), f32),
        ),
        in_specs=vmem(5),
        out_specs=tuple(vmem(5)),
        scratch_shapes=[pltpu.VMEM((length, LANES), f32)] * 2,
        compiler_params=params,
        name="scan",
    )(gated, parts, outer, decay, coef)


def heads_call(me, states, decay, coef, yf, yb, outer, back_sum):
    _, rows, width = outer.shape
    length = 2 * width
    return pl.pallas_call(
        heads_kernel,
        out_shape=(
            jax.ShapeDtypeStruct((rows, length), bf16),
            jax.ShapeDtypeStruct((2, rows, width), bf16),
            jax.ShapeDtypeStruct((2, rows, width), bf16),
        ),
        in_specs=[pl.BlockSpec(memory_space=pltpu.SMEM)] + vmem(7),
        out_specs=tuple(vmem(3)),
        scratch_shapes=[pltpu.VMEM((length, LANES), f32)] * 2,
        compiler_params=params,
        name="heads",
    )(me, states, decay, coef, yf, yb, outer, back_sum)


def swap(x, axes):
    return lax.all_to_all(x, axes, 0, 0, tiled=True)


def by_core(x):
    rows, n = x.shape
    return x.reshape(rows // (2 * SUB), 2, SUB, n).swapaxes(0, 1).reshape(2, rows // 2, n)


def from_cores(x):
    _, rows, n = x.shape
    return x.reshape(2, rows // SUB, SUB, n).swapaxes(0, 1).reshape(2 * rows, n)


def shards(outer_gate, inner_gate, value_proj, residues, decays, out_weight, out_grad):
    chan_rows, tok = outer_gate.shape
    half = chan_rows // 2
    cols = out_weight.shape[1]
    core = lax.axis_index("core")
    chip = lax.axis_index(("y", "zh"))
    chips = lax.axis_size(("y", "zh"))
    nx, nz = lax.axis_size("x"), lax.axis_size("zl")
    inner = inner_gate.astype(f32)
    value = value_proj.astype(f32)
    gated = (inner * value).astype(bf16)

    coef = residues * jnp.sqrt(-jnp.expm1(-2.0 * decays))

    def own_modes(x):
        x = lax.dynamic_index_in_dim(by_core(x), core, 0, keepdims=False)
        return jnp.pad(x.T, ((0, 0), (0, LANES - half)))

    decay, coef = own_modes(decays), own_modes(coef)

    sent = jnp.concatenate(
        [jnp.broadcast_to(out_grad[None], (2, tok, cols)), by_core(gated), by_core(outer_gate)], axis=1
    )
    got = swap(sent, "core")
    grads = got[:, :tok].reshape(2 * tok, cols)
    gated = got[:, tok : tok + half]
    outer = got[:, tok + half :]
    weight = lax.dynamic_index_in_dim(
        out_weight.reshape(-1, 2, SUB, cols), core, 1, keepdims=False
    ).reshape(-1, cols)

    back = lax.dot_general(weight, grads, (((1,), (1,)), ((), ())), preferred_element_type=f32)
    back = swap(back.astype(bf16), "x")
    back = jnp.sum(back.reshape(nx, -1, 2 * tok).astype(f32), axis=0).astype(bf16)
    back = swap(back, "zl").reshape(nz, half, 2 * tok)

    yf, yb, back_sum, sf, sb = scan_call(gated, back, outer, decay, coef)
    order = jnp.arange(chips)[:, None, None]
    states = swap(jnp.where(order > chip, sf[None], sb[None]), ("y", "zh"))
    me = jnp.full((1,), chip, jnp.int32)
    product, grad_outer, back_gated = heads_call(me, states, decay, coef, yf, yb, outer, back_sum)

    product = lax.all_gather(product, "zl", axis=0, tiled=True)
    product = swap(jnp.broadcast_to(product[None], (nx,) + product.shape).reshape(-1, 2 * tok), "x")
    mixed = lax.dot_general(product, weight, (((0,), (0,)), ((), ())), preferred_element_type=f32)
    grad_weight = jnp.dot(product, grads, preferred_element_type=f32).astype(bf16)
    grad_weight = swap(grad_weight, ("y", "zh")).reshape(chips, 2 * SUB, cols)
    scale = 1.0 / math.sqrt(2 * tok * chips)
    grad_weight = jnp.sum(grad_weight.astype(f32), axis=0) * scale

    sent = jnp.concatenate(
        [
            mixed.reshape(2, tok, cols),
            back_gated.astype(f32),
            grad_outer.astype(f32),
            grad_weight.reshape(2, SUB, cols),
        ],
        axis=1,
    )
    got = swap(sent, "core")
    mixed = (got[0, :tok] + got[1, :tok]).astype(bf16)
    back_gated = from_cores(got[:, tok : tok + half])
    grad_outer = from_cores(got[:, tok + half : tok + 2 * half]).astype(bf16)
    grad_weight = got[:, tok + 2 * half :].reshape(2 * SUB, cols)
    grad_inner = (back_gated * value).astype(bf16)
    grad_value = (back_gated * inner).astype(bf16)
    return (mixed, grad_outer, grad_inner, grad_value, grad_weight)


def solution(mesh):
    fine = Mesh(mesh.devices.reshape(8, 3, 2, 4, 4), ("y", "zh", "core", "x", "zl"))
    seq, col = ("y", "zh", "core"), ("x", "zl")
    return jax.shard_map(
        shards,
        mesh=fine,
        in_specs=(
            P(col, seq),
            P(col, seq),
            P(col, seq),
            P(col, None),
            P(col, None),
            P(None, col),
            P(seq, col),
        ),
        out_specs=(P(seq, col), P(col, seq), P(col, seq), P(col, seq), P(seq, col)),
        check_vma=False,
    )
```

```python
import math

import jax
import jax.numpy as jnp
from jax import lax
from jax.experimental import pallas as pl
from jax.experimental.pallas import tpu as pltpu
from jax.sharding import Mesh
from jax.sharding import PartitionSpec as P

f32 = jnp.float32
bf16 = jnp.bfloat16
SUB = 32
LANES = 128
CORE, X, CHIP = 0, 1, 2


def to_columns(tile):
    rows, width = tile.shape
    pad = jnp.zeros((LANES - rows, width), f32)
    return jnp.concatenate([tile, pad], axis=0).T


def pack_kernel(i_ref, v_ref, o_ref, g_ref, sent_ref):
    tok = g_ref.shape[0]
    rows = i_ref.shape[0]
    for h in range(2):
        sent_ref[h, :tok] = g_ref[...]
        for b in range(rows // (2 * SUB)):
            src = pl.ds(2 * SUB * b + SUB * h, SUB)
            gated = (i_ref[src, :].astype(f32) * v_ref[src, :].astype(f32)).astype(bf16)
            sent_ref[h, pl.ds(tok + SUB * b, SUB)] = gated
            sent_ref[h, pl.ds(tok + rows // 2 + SUB * b, SUB)] = o_ref[src, :]


def modes_kernel(at_ref, d_ref, c_ref, od_ref, oc_ref):
    chan = lax.broadcasted_iota(jnp.int32, (d_ref.shape[1], LANES), 0)
    lane = lax.broadcasted_iota(jnp.int32, (d_ref.shape[1], LANES), 1)
    wanted = lane + SUB * (lane // SUB) + SUB * at_ref[CORE]
    pick = jnp.where((chan == wanted) & (lane < d_ref.shape[1] // 2), 1.0, 0.0).astype(f32)
    for src, dst in ((d_ref, od_ref), (c_ref, oc_ref)):
        dst[...] = jnp.dot(
            src[...], pick, precision=lax.Precision.HIGHEST, preferred_element_type=f32
        )


def back_kernel(at_ref, w_ref, got_ref, own_ref, *sent_refs):
    tok = got_ref.shape[2]
    n = 1 + len(sent_refs)
    rows = w_ref.shape[0] // n
    for k, ref in enumerate((own_ref,) + sent_refs):
        block = lax.rem(at_ref[X] + k, n)
        w = w_ref[pl.ds(pl.multiple_of(block * rows, rows), rows), :]
        for h in range(2):
            part = lax.dot_general(
                w, got_ref[h, :tok], (((1,), (1,)), ((), ())), preferred_element_type=f32
            )
            ref[:, pl.ds(h * tok, tok)] = part.astype(ref.dtype)


def scan(src, y_ref, rate, coef, reverse):
    length = src.shape[0]

    def step(i, state):
        lo = length - 8 - i * 8 if reverse else i * 8
        at = pl.ds(pl.multiple_of(lo, 8), 8)
        block = src[at, :]
        rows = [None] * 8
        for t in range(8):
            u = 7 - t if reverse else t
            state = state * rate + block[u : u + 1, :]
            rows[u] = jnp.sum(state * coef, axis=0, keepdims=True)
        y_ref[at, :] = jnp.concatenate(rows, axis=0)
        return state

    return lax.fori_loop(0, length // 8, step, jnp.zeros_like(coef))


def heads(y_ref, out, state, rate, reverse):
    length = y_ref.shape[0]

    def step(i, state):
        lo = length - 8 - i * 8 if reverse else i * 8
        at = pl.ds(pl.multiple_of(lo, 8), 8)
        rows = [None] * 8
        for t in range(8):
            u = 7 - t if reverse else t
            state = state * rate
            rows[u] = jnp.sum(state, axis=0, keepdims=True)
        out[at, :] = y_ref[at, :] + jnp.concatenate(rows, axis=0)
        return state

    lax.fori_loop(0, length // 8, step, state)


def scan_forward_kernel(got_ref, d_ref, c_ref, y_ref, s_ref, gt):
    tok = got_ref.shape[2]
    half = (got_ref.shape[1] - tok) // 2
    for h in range(2):
        gt[pl.ds(h * tok, tok), :] = to_columns(got_ref[h, tok : tok + half].astype(f32))
    state = scan(gt, y_ref, jnp.exp(-d_ref[...]), c_ref[...], False)
    for m in range(s_ref.shape[0]):
        s_ref[m] = state


def meet_kernel(at_ref, s_ref, d_ref, c_ref, y_ref, got_ref, own_ref, r1, r2, r3, sent_ref, f_ref, ft):
    tok = got_ref.shape[2]
    nz, twice, length = sent_ref.shape
    half = twice // 2
    decay = d_ref[...]
    jump = jnp.exp(-decay * float(length))
    state = jnp.zeros_like(decay)
    for m in range(s_ref.shape[0]):
        state = jnp.where(m < at_ref[CHIP], state * jump + s_ref[m], state)
    heads(y_ref, ft, state * c_ref[...], jnp.exp(-decay), False)
    for h in range(2):
        at = pl.ds(h * tok, tok)
        filtered = ft[at, :].T[:half].astype(bf16)
        f_ref[h] = filtered
        product = (got_ref[h, tok + half :].astype(f32) * filtered.astype(f32)).astype(bf16)
        for q in range(nz):
            sent_ref[q, half:, at] = product
    for q in range(nz):
        rows = pl.ds(q * half, half)
        total = own_ref[rows, :]
        for ref in (r1, r2, r3):
            total = total + ref[rows, :].astype(f32)
        sent_ref[q, :half, :] = total.astype(bf16)


def scan_backward_kernel(z_ref, got_ref, d_ref, c_ref, y_ref, s_ref, b_ref, bt):
    tok = got_ref.shape[2]
    half = z_ref.shape[1] // 2
    for h in range(2):
        at = pl.ds(h * tok, tok)
        total = z_ref[0, :half, at].astype(f32)
        for q in range(1, z_ref.shape[0]):
            total = total + z_ref[q, :half, at].astype(f32)
        b_ref[h] = total
        outer = got_ref[h, tok + half :].astype(f32)
        bt[at, :] = to_columns((total * outer).astype(bf16).astype(f32))
    state = scan(bt, y_ref, jnp.exp(-d_ref[...]), c_ref[...], True)
    for m in range(s_ref.shape[0]):
        s_ref[m] = state


def weight_kernel(at_ref, p0, p1, p2, p3, got_ref, out_ref):
    tok = got_ref.shape[2]
    rows = p0.shape[0]
    grads = got_ref[:, :tok, :].reshape(2 * tok, -1)
    for k, piece in enumerate((p0, p1, p2, p3)):
        block = lax.rem(at_ref[X] + 4 - k, 4)
        at = pl.ds(pl.multiple_of(block * rows, rows), rows)
        out_ref[at, :] = jnp.dot(piece[...], grads, preferred_element_type=f32).astype(bf16)


def mixed_kernel(at_ref, p0, p1, p2, p3, w_ref, own_ref, other_ref, total):
    rows = p0.shape[0]
    tok = own_ref.shape[1]
    for k, piece in enumerate((p0, p1, p2, p3)):
        block = lax.rem(at_ref[X] + 4 - k, 4)
        w = w_ref[pl.ds(pl.multiple_of(block * rows, rows), rows), :]
        part = lax.dot_general(w, piece[...], (((0,), (0,)), ((), ())), preferred_element_type=f32)
        if k == 0:
            total[...] = part
        else:
            total[...] += part
    core = at_ref[CORE]
    own_ref[...] = total[:, pl.ds(pl.multiple_of(core * tok, tok), tok)]
    other_ref[...] = total[:, pl.ds(pl.multiple_of((1 - core) * tok, tok), tok)]


def heads_backward_kernel(at_ref, s_ref, d_ref, c_ref, y_ref, f_ref, b_ref, own_ref, other_ref, bt):
    half, tok = f_ref.shape[1:]
    decay = d_ref[...]
    jump = jnp.exp(-decay * float(2 * tok))
    state = jnp.zeros_like(decay)
    for m in range(s_ref.shape[0] - 1, -1, -1):
        state = jnp.where(m > at_ref[CHIP], state * jump + s_ref[m], state)
    heads(y_ref, bt, state * c_ref[...], jnp.exp(-decay), True)
    core = at_ref[CORE]
    for h, ref in ((core, own_ref), (1 - core, other_ref)):
        at = pl.ds(pl.multiple_of(h * tok, tok), tok)
        ref[:half] = bt[at, :].T[:half].astype(bf16)
        ref[half:] = (b_ref[h] * f_ref[h].astype(f32)).astype(bf16)


def finish_kernel(at_ref, m_ref, mr_ref, g_ref, gr_ref, i_ref, v_ref, mixed_ref, go_ref, gi_ref, gv_ref):
    mixed_ref[...] = (m_ref[...] + mr_ref[...]).T.astype(bf16)
    half = g_ref.shape[0] // 2
    core = at_ref[CORE]
    for h, ref in ((core, g_ref), (1 - core, gr_ref)):
        for b in range(half // SUB):
            at = pl.ds(pl.multiple_of(2 * SUB * b + SUB * h, SUB), SUB)
            back = ref[pl.ds(SUB * b, SUB), :].astype(f32)
            go_ref[at, :] = ref[pl.ds(half + SUB * b, SUB), :]
            gi_ref[at, :] = (back * v_ref[at, :].astype(f32)).astype(bf16)
            gv_ref[at, :] = (back * i_ref[at, :].astype(f32)).astype(bf16)


def total_kernel(scale, at_ref, p_ref, own_ref, other_ref):
    core = at_ref[CORE]
    for h, ref in ((core, own_ref), (1 - core, other_ref)):
        at = pl.ds(pl.multiple_of(h * SUB, SUB), SUB)
        total = p_ref[0, at, :].astype(f32)
        for m in range(1, p_ref.shape[0]):
            total = total + p_ref[m, at, :].astype(f32)
        ref[...] = total * scale


def join_kernel(at_ref, own_ref, other_ref, out_ref):
    core = at_ref[CORE]
    for h, ref in ((core, own_ref), (1 - core, other_ref)):
        out_ref[pl.ds(pl.multiple_of(h * SUB, SUB), SUB), :] = ref[...]


def whole(shape):
    return pl.BlockSpec(shape, lambda i: (0,) * len(shape))


def call(kernel, name, outs, args, scratch=(), indexed=True):
    specs = [whole(arg.shape) for arg in args]
    if indexed:
        specs[0] = pl.BlockSpec(memory_space=pltpu.SMEM)
    return pl.pallas_call(
        kernel,
        grid=(1,),
        out_shape=tuple(jax.ShapeDtypeStruct(s, t) for s, t in outs),
        in_specs=specs,
        out_specs=tuple(whole(s) for s, _ in outs),
        scratch_shapes=[pltpu.VMEM(s, f32) for s in scratch],
        compiler_params=pltpu.CompilerParams(vmem_limit_bytes=24 * 2**20),
        name=name,
    )(*args)


def swap(x, axes):
    return lax.all_to_all(x, axes, 0, 0, tiled=True)


def shift(x, axis, k):
    n = lax.axis_size(axis)
    return lax.ppermute(x, axis, [(i, (i + k) % n) for i in range(n)])


def shards(outer_gate, inner_gate, value_proj, residues, decays, out_weight, out_grad):
    chan, tok = outer_gate.shape
    half = chan // 2
    length = 2 * tok
    cols = out_weight.shape[1]
    modes = decays.shape[1]
    core = lax.axis_index("core")
    chips = lax.axis_size(("y", "zh"))
    nx, nz = lax.axis_size("x"), lax.axis_size("zl")
    at = jnp.stack([core, lax.axis_index("x"), lax.axis_index(("y", "zh"))]).astype(jnp.int32)

    (sent,) = call(
        pack_kernel,
        "pack",
        [((2, tok + chan, cols), bf16)],
        (inner_gate, value_proj, outer_gate, out_grad),
        indexed=False,
    )
    got = swap(sent, "core")

    coef = residues * jnp.sqrt(-jnp.expm1(-2.0 * decays))
    small = ((modes, LANES), f32)
    decay, coef = call(modes_kernel, "modes", [small, small], (at, decays.T, coef.T))
    weight = lax.dynamic_index_in_dim(
        out_weight.reshape(-1, 2, SUB, cols), core, 1, keepdims=False
    ).reshape(-1, cols)

    rows = nz * half
    own, *parts = call(
        back_kernel,
        "back",
        [((rows, length), f32)] + [((rows, length), bf16)] * (nx - 1),
        (at, weight, got),
    )
    parts = [shift(part, "x", k + 1) for k, part in enumerate(parts)]
    columns = ((length, LANES), f32)
    states = ((chips, modes, LANES), f32)
    y, s = call(
        scan_forward_kernel,
        "scan_forward",
        [columns, states],
        (got, decay, coef),
        scratch=[(length, LANES)],
        indexed=False,
    )
    s = swap(s, ("y", "zh"))
    sent, filtered = call(
        meet_kernel,
        "meet",
        [((nz, chan, length), bf16), ((2, half, tok), bf16)],
        (at, s, decay, coef, y, got, own, *parts),
        scratch=[(length, LANES)],
    )
    both = swap(sent, "zl")

    piece = both[:, half:].reshape(rows, length)
    pieces = [piece] + [shift(piece, "x", k) for k in range(1, nx)]
    y, s, back_sum = call(
        scan_backward_kernel,
        "scan_backward",
        [columns, states, ((2, half, tok), f32)],
        (both, got, decay, coef),
        scratch=[(length, LANES)],
        indexed=False,
    )
    s = swap(s, ("y", "zh"))

    (partial,) = call(
        weight_kernel, "weight", [((nx * rows, cols), bf16)], (at, *pieces, got)
    )
    partial = swap(partial, ("y", "zh")).reshape(chips, 2 * SUB, cols)

    grads, grads_other = call(
        heads_backward_kernel,
        "heads_backward",
        [((chan, tok), bf16)] * 2,
        (at, s, decay, coef, y, filtered, back_sum),
        scratch=[(length, LANES)],
    )
    mixed, mixed_other = call(
        mixed_kernel,
        "mixed",
        [((cols, tok), f32)] * 2,
        (at, *pieces, weight),
        scratch=[(cols, length)],
    )
    mixed, grad_outer, grad_inner, grad_value = call(
        finish_kernel,
        "finish",
        [((tok, cols), bf16)] + [((chan, tok), bf16)] * 3,
        (
            at,
            mixed,
            shift(mixed_other, "core", 1),
            grads,
            shift(grads_other, "core", 1),
            inner_gate,
            value_proj,
        ),
    )

    scale = 1.0 / math.sqrt(length * chips)
    own, other = call(
        lambda *refs: total_kernel(scale, *refs),
        "total",
        [((SUB, cols), f32)] * 2,
        (at, partial),
    )
    (grad_weight,) = call(
        join_kernel, "join", [((2 * SUB, cols), f32)], (at, own, shift(other, "core", 1))
    )
    return (mixed, grad_outer, grad_inner, grad_value, grad_weight)


def solution(mesh):
    fine = Mesh(mesh.devices.reshape(8, 3, 2, 4, 4), ("y", "zh", "core", "x", "zl"))
    seq, col = ("y", "zh", "core"), ("x", "zl")
    return jax.shard_map(
        shards,
        mesh=fine,
        in_specs=(
            P(col, seq),
            P(col, seq),
            P(col, seq),
            P(col, None),
            P(col, None),
            P(None, col),
            P(seq, col),
        ),
        out_specs=(P(seq, col), P(col, seq), P(col, seq), P(col, seq), P(seq, col)),
        check_vma=False,
    )
```

```python
import math

import jax
import jax.numpy as jnp
from jax import lax
from jax.experimental import pallas as pl
from jax.experimental.pallas import tpu as pltpu
from jax.sharding import Mesh
from jax.sharding import PartitionSpec as P

f32 = jnp.float32
bf16 = jnp.bfloat16
SUB = 32
LANES = 128
CORE, X, CHIP = 0, 1, 2


def to_columns(tile):
    rows, width = tile.shape
    pad = jnp.zeros((LANES - rows, width), f32)
    return jnp.concatenate([tile, pad], axis=0).T


def back_kernel(w_ref, g_ref, out_ref):
    chan = 6 * SUB
    grads = g_ref[...]
    for j in range(w_ref.shape[0] // chan):
        part = lax.dot_general(
            w_ref[pl.ds(j * chan, chan), :],
            grads,
            (((1,), (1,)), ((), ())),
            preferred_element_type=f32,
        ).astype(bf16)
        for b in range(6):
            dst = j * chan + (b % 2) * 3 * SUB + (b // 2) * SUB
            out_ref[pl.ds(dst, SUB), :] = part[b * SUB : (b + 1) * SUB]


def pack_kernel(at_ref, i_ref, v_ref, o_ref, g_ref, own_ref, other_ref):
    tok = g_ref.shape[0]
    half = i_ref.shape[0] // 2
    core = at_ref[CORE]
    for h, ref in ((core, own_ref), (1 - core, other_ref)):
        ref[:tok] = g_ref[...]
        for b in range(half // SUB):
            src = pl.ds(pl.multiple_of(2 * SUB * b + SUB * h, SUB), SUB)
            gated = (i_ref[src, :].astype(f32) * v_ref[src, :].astype(f32)).astype(bf16)
            ref[pl.ds(tok + SUB * b, SUB), :] = gated
            ref[pl.ds(tok + half + SUB * b, SUB), :] = o_ref[src, :]


def both_kernel(at_ref, own_ref, other_ref, out_ref):
    core = at_ref[CORE]
    out_ref[core] = own_ref[...]
    out_ref[1 - core] = other_ref[...]


def modes_kernel(at_ref, d_ref, c_ref, od_ref, oc_ref):
    chan = lax.broadcasted_iota(jnp.int32, (d_ref.shape[1], LANES), 0)
    lane = lax.broadcasted_iota(jnp.int32, (d_ref.shape[1], LANES), 1)
    wanted = lane + SUB * (lane // SUB) + SUB * at_ref[CORE]
    pick = jnp.where((chan == wanted) & (lane < d_ref.shape[1] // 2), 1.0, 0.0).astype(f32)
    for src, dst in ((d_ref, od_ref), (c_ref, oc_ref)):
        dst[...] = jnp.dot(
            src[...], pick, precision=lax.Precision.HIGHEST, preferred_element_type=f32
        )


def sum_kernel(p_ref, out_ref):
    total = p_ref[0].astype(f32)
    for i in range(1, p_ref.shape[0]):
        total = total + p_ref[i].astype(f32)
    out_ref[...] = total.astype(bf16)


def scan_kernel(at_ref, got_ref, z_ref, d_ref, c_ref, yf_ref, yb_ref, bs_ref, s_ref, gt, bt):
    tok = got_ref.shape[2]
    half = (got_ref.shape[1] - tok) // 2
    for h in range(2):
        at = pl.ds(h * tok, tok)
        gt[at, :] = to_columns(got_ref[h, tok : tok + half].astype(f32))
        total = z_ref[0, h].astype(f32)
        for q in range(1, z_ref.shape[0]):
            total = total + z_ref[q, h].astype(f32)
        bs_ref[h] = total
        outer = got_ref[h, tok + half :].astype(f32)
        bt[at, :] = to_columns((total * outer).astype(bf16).astype(f32))
    rate = jnp.exp(-d_ref[...])
    coef = c_ref[...]
    length = gt.shape[0]

    def step(i, carry):
        sf, sb = carry
        lo = pl.ds(pl.multiple_of(i * 8, 8), 8)
        hi = pl.ds(pl.multiple_of(length - 8 - i * 8, 8), 8)
        gs, bs = gt[lo, :], bt[hi, :]
        fs, rs = [], [None] * 8
        for t in range(8):
            sf = sf * rate + gs[t : t + 1, :]
            sb = sb * rate + bs[7 - t : 8 - t, :]
            fs.append(jnp.sum(sf * coef, axis=0, keepdims=True))
            rs[7 - t] = jnp.sum(sb * coef, axis=0, keepdims=True)
        yf_ref[lo, :] = jnp.concatenate(fs, axis=0)
        yb_ref[hi, :] = jnp.concatenate(rs, axis=0)
        return sf, sb

    zero = jnp.zeros_like(coef)
    sf, sb = lax.fori_loop(0, length // 8, step, (zero, zero))
    for m in range(s_ref.shape[0]):
        s_ref[m] = jnp.where(m > at_ref[CHIP], sf, sb)


def heads_kernel(at_ref, s_ref, d_ref, c_ref, yf_ref, yb_ref, got_ref, bs_ref, p_ref, own_ref, other_ref, ft, bt):
    me = at_ref[CHIP]
    tok = got_ref.shape[2]
    half = (got_ref.shape[1] - tok) // 2
    decay = d_ref[...]
    rate = jnp.exp(-decay)
    coef = c_ref[...]
    length = ft.shape[0]
    chips = s_ref.shape[0]
    jump = jnp.exp(-decay * float(length))
    pf = jnp.zeros_like(coef)
    pb = jnp.zeros_like(coef)
    for m in range(chips):
        pf = jnp.where(m < me, pf * jump + s_ref[m], pf)
        back = chips - 1 - m
        pb = jnp.where(back > me, pb * jump + s_ref[back], pb)

    def step(i, carry):
        pf, pb = carry
        lo = pl.ds(pl.multiple_of(i * 8, 8), 8)
        hi = pl.ds(pl.multiple_of(length - 8 - i * 8, 8), 8)
        fs, rs = [], [None] * 8
        for t in range(8):
            pf = pf * rate
            pb = pb * rate
            fs.append(jnp.sum(pf, axis=0, keepdims=True))
            rs[7 - t] = jnp.sum(pb, axis=0, keepdims=True)
        ft[lo, :] = yf_ref[lo, :] + jnp.concatenate(fs, axis=0)
        bt[hi, :] = yb_ref[hi, :] + jnp.concatenate(rs, axis=0)
        return pf, pb

    lax.fori_loop(0, length // 8, step, (pf * coef, pb * coef))
    core = at_ref[CORE]
    for h, ref in ((core, own_ref), (1 - core, other_ref)):
        at = pl.ds(pl.multiple_of(h * tok, tok), tok)
        filtered = ft[at, :].T[:half].astype(bf16).astype(f32)
        product = (got_ref[h, tok + half :].astype(f32) * filtered).astype(bf16)
        for q in range(p_ref.shape[0]):
            p_ref[q, :, at] = product
        ref[:half] = bt[at, :].T[:half].astype(bf16)
        ref[half:] = (bs_ref[h] * filtered).astype(bf16)


def weight_kernel(p_ref, got_ref, out_ref):
    tok = got_ref.shape[2]
    grads = got_ref[:, :tok, :].reshape(2 * tok, -1)
    out_ref[...] = jnp.dot(p_ref[...], grads, preferred_element_type=f32).astype(bf16)


def mixed_kernel(at_ref, p_ref, w_ref, own_ref, other_ref, total):
    tok = own_ref.shape[1]
    total[...] = lax.dot_general(
        w_ref[...], p_ref[...], (((0,), (0,)), ((), ())), preferred_element_type=f32
    )
    core = at_ref[CORE]
    own_ref[...] = total[:, pl.ds(pl.multiple_of(core * tok, tok), tok)]
    other_ref[...] = total[:, pl.ds(pl.multiple_of((1 - core) * tok, tok), tok)]


def finish_kernel(at_ref, m_ref, mr_ref, g_ref, gr_ref, i_ref, v_ref, mixed_ref, go_ref, gi_ref, gv_ref):
    mixed_ref[...] = (m_ref[...] + mr_ref[...]).T.astype(bf16)
    half = g_ref.shape[0] // 2
    core = at_ref[CORE]
    for h, ref in ((core, g_ref), (1 - core, gr_ref)):
        for b in range(half // SUB):
            at = pl.ds(pl.multiple_of(2 * SUB * b + SUB * h, SUB), SUB)
            back = ref[pl.ds(SUB * b, SUB), :].astype(f32)
            go_ref[at, :] = ref[pl.ds(half + SUB * b, SUB), :]
            gi_ref[at, :] = (back * v_ref[at, :].astype(f32)).astype(bf16)
            gv_ref[at, :] = (back * i_ref[at, :].astype(f32)).astype(bf16)


def total_kernel(scale, p_ref, out_ref):
    for h in range(2):
        total = p_ref[h].astype(f32)
        for m in range(1, p_ref.shape[0] // 2):
            total = total + p_ref[2 * m + h].astype(f32)
        out_ref[pl.ds(h * SUB, SUB), :] = total * scale


def call(kernel, name, outs, args, scratch=(), indexed=True):
    specs = [pl.BlockSpec(memory_space=pltpu.VMEM)] * len(args)
    if indexed:
        specs[0] = pl.BlockSpec(memory_space=pltpu.SMEM)
    return pl.pallas_call(
        kernel,
        out_shape=tuple(jax.ShapeDtypeStruct(s, t) for s, t in outs),
        in_specs=specs,
        out_specs=tuple([pl.BlockSpec(memory_space=pltpu.VMEM)] * len(outs)),
        scratch_shapes=[pltpu.VMEM(s, f32) for s in scratch],
        compiler_params=pltpu.CompilerParams(vmem_limit_bytes=24 * 2**20),
        name=name,
    )(*args)


def swap(x, axes):
    return lax.all_to_all(x, axes, 0, 0, tiled=True)


def spread(x, axis):
    n, rows, m = x.shape
    return swap(x.reshape(n * rows, m), axis)


def other_core(x):
    return lax.ppermute(x, "core", [(0, 1), (1, 0)])


def shards(outer_gate, inner_gate, value_proj, residues, decays, out_weight, out_grad):
    chan, tok = outer_gate.shape
    half = chan // 2
    length = 2 * tok
    all_chan, cols = out_weight.shape
    modes = decays.shape[1]
    core = lax.axis_index("core")
    chips = lax.axis_size(("y", "zh"))
    nx, nz = lax.axis_size("x"), lax.axis_size("zl")
    at = jnp.stack([core, lax.axis_index("x"), lax.axis_index(("y", "zh"))]).astype(jnp.int32)

    (part,) = call(
        back_kernel, "back", [((all_chan, tok), bf16)], (out_weight, out_grad), indexed=False
    )
    part = swap(part, "x").reshape(nx, all_chan // nx, tok)

    own, other = call(
        pack_kernel,
        "pack",
        [((tok + chan, cols), bf16)] * 2,
        (at, inner_gate, value_proj, outer_gate, out_grad),
    )
    (got,) = call(
        both_kernel, "both", [((2, tok + chan, cols), bf16)], (at, own, other_core(other))
    )
    coef = residues * jnp.sqrt(-jnp.expm1(-2.0 * decays))
    small = ((modes, LANES), f32)
    decay, coef = call(modes_kernel, "modes", [small, small], (at, decays.T, coef.T))
    weight = lax.dynamic_index_in_dim(
        out_weight.reshape(-1, 2, SUB, cols), core, 1, keepdims=False
    ).reshape(-1, cols)

    (part,) = call(sum_kernel, "sum", [((all_chan // nx, tok), bf16)], (part,), indexed=False)
    part = swap(part, ("zl", "core")).reshape(nz, 2, half, tok)

    columns = ((length, LANES), f32)
    yf, yb, back_sum, states = call(
        scan_kernel,
        "scan",
        [columns, columns, ((2, half, tok), f32), ((chips, modes, LANES), f32)],
        (at, got, part, decay, coef),
        scratch=[(length, LANES)] * 2,
    )
    states = swap(states, ("y", "zh"))
    product, grads, grads_other = call(
        heads_kernel,
        "heads",
        [((nz, half, length), bf16)] + [((chan, tok), bf16)] * 2,
        (at, states, decay, coef, yf, yb, got, back_sum),
        scratch=[(length, LANES)] * 2,
    )
    product = spread(product, "zl")
    product = spread(jnp.broadcast_to(product[None], (nx,) + product.shape), "x")

    (partial,) = call(
        weight_kernel,
        "weight",
        [((product.shape[0], cols), bf16)],
        (product, got),
        indexed=False,
    )
    partial = swap(partial, ("y", "zh", "core")).reshape(2 * chips, SUB, cols)

    mixed, mixed_other = call(
        mixed_kernel,
        "mixed",
        [((cols, tok), f32)] * 2,
        (at, product, weight),
        scratch=[(cols, length)],
    )
    outs = call(
        finish_kernel,
        "finish",
        [((tok, cols), bf16)] + [((chan, tok), bf16)] * 3,
        (
            at,
            mixed,
            other_core(mixed_other),
            grads,
            other_core(grads_other),
            inner_gate,
            value_proj,
        ),
    )
    *outs, partial = lax.optimization_barrier((*outs, partial))
    scale = 1.0 / math.sqrt(length * chips)
    (grad_weight,) = call(
        lambda *refs: total_kernel(scale, *refs),
        "total",
        [((2 * SUB, cols), f32)],
        (partial,),
        indexed=False,
    )
    return (*outs, grad_weight)


def solution(mesh):
    fine = Mesh(mesh.devices.reshape(8, 3, 2, 4, 4), ("y", "zh", "core", "x", "zl"))
    seq, col = ("y", "zh", "core"), ("x", "zl")
    return jax.shard_map(
        shards,
        mesh=fine,
        in_specs=(
            P(col, seq),
            P(col, seq),
            P(col, seq),
            P(col, None),
            P(col, None),
            P(None, col),
            P(seq, col),
        ),
        out_specs=(P(seq, col), P(col, seq), P(col, seq), P(col, seq), P(seq, col)),
        check_vma=False,
    )
```

```python
import math

import jax
import jax.numpy as jnp
from jax import lax
from jax.experimental import pallas as pl
from jax.experimental.pallas import tpu as pltpu
from jax.sharding import Mesh
from jax.sharding import PartitionSpec as P

f32 = jnp.float32
bf16 = jnp.bfloat16
SUB = 32
LANES = 128
CORE, X, ZL, CHIP = "core", "x", "zl", ("y", "zh")


def to_columns(tile):
    rows, width = tile.shape
    pad = jnp.zeros((LANES - rows, width), f32)
    return jnp.concatenate([tile, pad], axis=0).T


def pack_kernel(i_hbm, v_hbm, o_hbm, g_hbm, own_ref, other_ref, i_ref, v_ref, o_ref, g_ref, sems):
    copies = [
        pltpu.make_async_copy(src, dst, sems.at[k])
        for k, (src, dst) in enumerate(
            ((i_hbm, i_ref), (v_hbm, v_ref), (o_hbm, o_ref), (g_hbm, g_ref))
        )
    ]
    for copy in copies:
        copy.start()
    for copy in copies:
        copy.wait()
    tok = g_ref.shape[0]
    half = i_ref.shape[0] // 2
    core = lax.axis_index(CORE)
    for h, ref in ((core, own_ref), (1 - core, other_ref)):
        ref[:tok] = g_ref[...]
        for b in range(half // SUB):
            src = pl.ds(pl.multiple_of(2 * SUB * b + SUB * h, SUB), SUB)
            gated = (i_ref[src, :].astype(f32) * v_ref[src, :].astype(f32)).astype(bf16)
            ref[pl.ds(tok + SUB * b, SUB), :] = gated
            ref[pl.ds(tok + half + SUB * b, SUB), :] = o_ref[src, :]


def both_kernel(own_ref, other_ref, out_ref):
    core = lax.axis_index(CORE)
    out_ref[core] = own_ref[...]
    out_ref[1 - core] = other_ref[...]


def modes_kernel(d_ref, c_ref, od_ref, oc_ref):
    chan = lax.broadcasted_iota(jnp.int32, (d_ref.shape[1], LANES), 0)
    lane = lax.broadcasted_iota(jnp.int32, (d_ref.shape[1], LANES), 1)
    wanted = lane + SUB * (lane // SUB) + SUB * lax.axis_index(CORE)
    pick = jnp.where((chan == wanted) & (lane < d_ref.shape[1] // 2), 1.0, 0.0).astype(f32)
    for src, dst in ((d_ref, od_ref), (c_ref, oc_ref)):
        dst[...] = jnp.dot(
            src[...], pick, precision=lax.Precision.HIGHEST, preferred_element_type=f32
        )


def weight_rows(w_ref, core, block, count):
    blocks = w_ref.shape[0] // (2 * SUB * count)
    rows = []
    for b in range(blocks):
        start = 2 * SUB * (block * blocks + b) + SUB * core
        rows.append(w_ref[pl.ds(pl.multiple_of(start, SUB), SUB), :])
    return jnp.concatenate(rows, axis=0)


def back_kernel(w_ref, got_ref, own_ref, *sent_refs):
    tok = got_ref.shape[2]
    n = 1 + len(sent_refs)
    for k, ref in enumerate((own_ref,) + sent_refs):
        w = weight_rows(w_ref, lax.axis_index(CORE), lax.rem(lax.axis_index(X) + k, n), n)
        for h in range(2):
            part = lax.dot_general(
                w, got_ref[h, :tok], (((1,), (1,)), ((), ())), preferred_element_type=f32
            )
            ref[:, pl.ds(h * tok, tok)] = part.astype(ref.dtype)


def sum_kernel(p0, p1, p2, p3, own_ref, *sent_refs):
    rows = own_ref.shape[0]
    n = 1 + len(sent_refs)
    for k, ref in enumerate((own_ref,) + sent_refs):
        block = lax.rem(lax.axis_index(ZL) + k, n)
        at = pl.ds(pl.multiple_of(block * rows, rows), rows)
        total = p0[at, :] + p1[at, :].astype(f32) + p2[at, :].astype(f32) + p3[at, :].astype(f32)
        ref[...] = total.astype(ref.dtype)


def scan(src, y_ref, rate, coef, reverse):
    length = src.shape[0]

    def step(i, state):
        lo = length - 8 - i * 8 if reverse else i * 8
        at = pl.ds(pl.multiple_of(lo, 8), 8)
        block = src[at, :]
        rows = [None] * 8
        for t in range(8):
            u = 7 - t if reverse else t
            state = state * rate + block[u : u + 1, :]
            rows[u] = jnp.sum(state * coef, axis=0, keepdims=True)
        y_ref[at, :] = jnp.concatenate(rows, axis=0)
        return state

    return lax.fori_loop(0, length // 8, step, jnp.zeros_like(coef))


def heads(y_ref, out, state, rate, reverse):
    length = y_ref.shape[0]

    def step(i, state):
        lo = length - 8 - i * 8 if reverse else i * 8
        at = pl.ds(pl.multiple_of(lo, 8), 8)
        rows = [None] * 8
        for t in range(8):
            u = 7 - t if reverse else t
            state = state * rate
            rows[u] = jnp.sum(state, axis=0, keepdims=True)
        out[at, :] = y_ref[at, :] + jnp.concatenate(rows, axis=0)
        return state

    lax.fori_loop(0, length // 8, step, state)


def scan_forward_kernel(got_ref, d_ref, c_ref, y_ref, s_ref, gt):
    tok = got_ref.shape[2]
    half = (got_ref.shape[1] - tok) // 2
    for h in range(2):
        gt[pl.ds(h * tok, tok), :] = to_columns(got_ref[h, tok : tok + half].astype(f32))
    state = scan(gt, y_ref, jnp.exp(-d_ref[...]), c_ref[...], False)
    for m in range(s_ref.shape[0]):
        s_ref[m] = state


def heads_forward_kernel(s_ref, d_ref, c_ref, y_ref, got_ref, p_ref, f_ref, ft):
    tok = got_ref.shape[2]
    half = f_ref.shape[1]
    decay = d_ref[...]
    jump = jnp.exp(-decay * float(ft.shape[0]))
    state = jnp.zeros_like(decay)
    for m in range(s_ref.shape[0]):
        state = jnp.where(m < lax.axis_index(CHIP), state * jump + s_ref[m], state)
    heads(y_ref, ft, state * c_ref[...], jnp.exp(-decay), False)
    for h in range(2):
        at = pl.ds(h * tok, tok)
        filtered = ft[at, :].T[:half].astype(bf16)
        f_ref[h] = filtered
        product = (got_ref[h, tok + half :].astype(f32) * filtered.astype(f32)).astype(bf16)
        for q in range(p_ref.shape[0]):
            p_ref[q, :, at] = product


def scan_backward_kernel(p0, p1, p2, p3, got_ref, d_ref, c_ref, y_ref, s_ref, b_ref, bt):
    tok = got_ref.shape[2]
    half = p0.shape[0]
    for h in range(2):
        at = pl.ds(h * tok, tok)
        total = p0[:, at] + p1[:, at].astype(f32) + p2[:, at].astype(f32) + p3[:, at].astype(f32)
        b_ref[h] = total
        outer = got_ref[h, tok + half :].astype(f32)
        bt[at, :] = to_columns((total * outer).astype(bf16).astype(f32))
    state = scan(bt, y_ref, jnp.exp(-d_ref[...]), c_ref[...], True)
    first = state.astype(bf16)
    s_ref[:, :LANES] = first
    s_ref[:, LANES:] = (state - first.astype(f32)).astype(bf16)


def weight_kernel(p_ref, got_ref, s_ref, out_ref):
    tok = got_ref.shape[2]
    chips = out_ref.shape[0]
    grads = got_ref[:, :tok, :].reshape(2 * tok, -1)
    part = jnp.dot(p_ref[...], grads, preferred_element_type=f32).astype(bf16)
    out_ref[:, : 2 * SUB, :] = part.reshape(chips, 2 * SUB, -1)
    for m in range(chips):
        out_ref[m, 2 * SUB :, :] = s_ref[...]


def mixed_kernel(p_ref, w_ref, own_ref, other_ref, total):
    tok = own_ref.shape[1]
    total[...] = lax.dot_general(
        weight_rows(w_ref, lax.axis_index(CORE), 0, 1),
        p_ref[...],
        (((0,), (0,)), ((), ())),
        preferred_element_type=f32,
    )
    core = lax.axis_index(CORE)
    own_ref[...] = total[:, pl.ds(pl.multiple_of(core * tok, tok), tok)]
    other_ref[...] = total[:, pl.ds(pl.multiple_of((1 - core) * tok, tok), tok)]


def last_kernel(scale, t_ref, d_ref, c_ref, y_ref, f_ref, b_ref, own_ref, other_ref, bt):
    half, tok = f_ref.shape[1:]
    rows = 2 * SUB
    decay = d_ref[...]
    jump = jnp.exp(-decay * float(2 * tok))
    state = jnp.zeros_like(decay)
    for m in range(t_ref.shape[0] - 1, -1, -1):
        two = t_ref[m, rows:, :].astype(f32)
        state = jnp.where(
            m > lax.axis_index(CHIP), state * jump + (two[:, :LANES] + two[:, LANES:]), state
        )
    heads(y_ref, bt, state * c_ref[...], jnp.exp(-decay), True)
    core = lax.axis_index(CORE)
    for h, ref in ((core, own_ref), (1 - core, other_ref)):
        at = pl.ds(pl.multiple_of(h * tok, tok), tok)
        ref[:half] = bt[at, :].T[:half].astype(bf16).astype(f32)
        ref[half : 2 * half] = (b_ref[h] * f_ref[h].astype(f32)).astype(bf16).astype(f32)
        mine = pl.ds(pl.multiple_of(h * SUB, SUB), SUB)
        total = t_ref[0, mine, :].astype(f32)
        for m in range(1, t_ref.shape[0]):
            total = total + t_ref[m, mine, :].astype(f32)
        ref[2 * half :] = total * scale


def finish_kernel(m_ref, mr_ref, own_ref, other_ref, i_ref, v_ref, mixed_ref, go_ref, gi_ref, gv_ref, gw_ref):
    mixed_ref[...] = (m_ref[...] + mr_ref[...]).T.astype(bf16)
    half = i_ref.shape[0] // 2
    core = lax.axis_index(CORE)
    for h, ref in ((core, own_ref), (1 - core, other_ref)):
        for b in range(half // SUB):
            at = pl.ds(pl.multiple_of(2 * SUB * b + SUB * h, SUB), SUB)
            back = ref[pl.ds(SUB * b, SUB), :]
            go_ref[at, :] = ref[pl.ds(half + SUB * b, SUB), :].astype(bf16)
            gi_ref[at, :] = (back * v_ref[at, :].astype(f32)).astype(bf16)
            gv_ref[at, :] = (back * i_ref[at, :].astype(f32)).astype(bf16)
        gw_ref[pl.ds(pl.multiple_of(SUB * h, SUB), SUB), :] = ref[2 * half :]


def call(kernel, name, outs, args, scratch=(), cost=None):
    specs = [pl.BlockSpec(memory_space=pltpu.VMEM)] * len(args)
    return pl.pallas_call(
        kernel,
        out_shape=tuple(jax.ShapeDtypeStruct(s, t) for s, t in outs),
        in_specs=specs,
        out_specs=tuple([pl.BlockSpec(memory_space=pltpu.VMEM)] * len(outs)),
        scratch_shapes=[pltpu.VMEM(s, f32) for s in scratch],
        compiler_params=pltpu.CompilerParams(vmem_limit_bytes=24 * 2**20),
        cost_estimate=cost,
        name=name,
    )(*args)


LONG = pl.CostEstimate(flops=10**11, bytes_accessed=0, transcendentals=0)


def swap(x, axes):
    return lax.all_to_all(x, axes, 0, 0, tiled=True)


def spread(x, axis):
    n, rows, m = x.shape
    return swap(x.reshape(n * rows, m), axis)


def shift(x, axis, k):
    n = lax.axis_size(axis)
    return lax.ppermute(x, axis, [(i, (i + k) % n) for i in range(n)])


def other_core(x):
    return lax.ppermute(x, "core", [(0, 1), (1, 0)])


def shards(outer_gate, inner_gate, value_proj, residues, decays, out_weight, out_grad):
    chan, tok = outer_gate.shape
    half = chan // 2
    length = 2 * tok
    all_chan, cols = out_weight.shape
    modes = decays.shape[1]
    chips = lax.axis_size(("y", "zh"))
    nx, nz = lax.axis_size("x"), lax.axis_size("zl")

    packed = ((tok + chan, cols), bf16)
    vmem = pl.BlockSpec(memory_space=pltpu.VMEM)
    anywhere = pl.BlockSpec(memory_space=pl.ANY)
    own, other = pl.pallas_call(
        pack_kernel,
        out_shape=(jax.ShapeDtypeStruct(*packed),) * 2,
        in_specs=[anywhere] * 4,
        out_specs=(vmem,) * 2,
        scratch_shapes=[pltpu.VMEM((chan, tok), bf16)] * 3
        + [pltpu.VMEM((tok, cols), bf16), pltpu.SemaphoreType.DMA((4,))],
        name="pack",
    )(inner_gate, value_proj, outer_gate, out_grad)
    (got,) = call(
        both_kernel, "both", [((2, tok + chan, cols), bf16)], (own, other_core(other))
    )
    coef = residues * jnp.sqrt(-jnp.expm1(-2.0 * decays))
    small = ((modes, LANES), f32)
    decay, coef = call(modes_kernel, "modes", [small, small], (decays.T, coef.T))

    rows = nz * half
    parts = call(
        back_kernel,
        "back",
        [((rows, length), f32)] + [((rows, length), bf16)] * (nx - 1),
        (out_weight, got),
    )
    got, own = lax.optimization_barrier((got, parts[0]))
    parts = [own] + [shift(part, "x", k) for k, part in enumerate(parts) if k]
    columns = ((length, LANES), f32)
    yf, states = call(
        scan_forward_kernel,
        "scan_forward",
        [columns, ((chips, modes, LANES), f32)],
        (got, decay, coef),
        scratch=[(length, LANES)],
    )
    states = swap(states, ("y", "zh"))
    parts = call(
        sum_kernel,
        "sum",
        [((half, length), f32)] + [((half, length), bf16)] * (nz - 1),
        parts,
        cost=LONG,
    )
    states, *parts = lax.optimization_barrier((states, *parts))
    product, filtered = call(
        heads_forward_kernel,
        "heads_forward",
        [((nz, half, length), bf16), ((2, half, tok), bf16)],
        (states, decay, coef, yf, got),
        scratch=[(length, LANES)],
    )
    product = spread(product, "zl")

    *parts, product = lax.optimization_barrier((*parts, product))
    parts = [parts[0]] + [shift(part, "zl", k) for k, part in enumerate(parts) if k]
    product = spread(jnp.broadcast_to(product[None], (nx,) + product.shape), "x")
    yb, state, back_sum = call(
        scan_backward_kernel,
        "scan_backward",
        [columns, ((modes, 2 * LANES), bf16), ((2, half, tok), f32)],
        (*parts, got, decay, coef),
        scratch=[(length, LANES)],
    )

    (partial,) = call(
        weight_kernel,
        "weight",
        [((chips, 2 * SUB + modes, cols), bf16)],
        (product, got, state),
    )
    partial = swap(partial, ("y", "zh"))
    mixed, mixed_other = call(
        mixed_kernel,
        "mixed",
        [((cols, tok), f32)] * 2,
        (product, out_weight),
        scratch=[(cols, length)],
    )
    mixed_other = other_core(mixed_other)
    scale = 1.0 / math.sqrt(length * chips)
    own, other = call(
        lambda *refs: last_kernel(scale, *refs),
        "last",
        [((chan + SUB, cols), f32)] * 2,
        (partial, decay, coef, yb, filtered, back_sum),
        scratch=[(length, LANES)],
    )
    return call(
        finish_kernel,
        "finish",
        [((tok, cols), bf16)] + [((chan, tok), bf16)] * 3 + [((2 * SUB, cols), f32)],
        (mixed, mixed_other, own, other_core(other), inner_gate, value_proj),
    )


def solution(mesh):
    fine = Mesh(mesh.devices.reshape(8, 3, 2, 4, 4), ("y", "zh", "core", "x", "zl"))
    seq, col = ("y", "zh", "core"), ("x", "zl")
    return jax.shard_map(
        shards,
        mesh=fine,
        in_specs=(
            P(col, seq),
            P(col, seq),
            P(col, seq),
            P(col, None),
            P(col, None),
            P(None, col),
            P(seq, col),
        ),
        out_specs=(P(seq, col), P(col, seq), P(col, seq), P(col, seq), P(seq, col)),
        check_vma=False,
    )
```

```python
import math

import jax
import jax.numpy as jnp
from jax import lax
from jax.experimental import pallas as pl
from jax.experimental.pallas import tpu as pltpu
from jax.sharding import Mesh
from jax.sharding import PartitionSpec as P

f32 = jnp.float32
bf16 = jnp.bfloat16
SUB = 32
LANES = 128
CORE, ZL, Y, ZH, CHIP = "core", "zl", "y", "zh", ("y", "zh")


def to_columns(tile):
    rows, width = tile.shape
    pad = jnp.zeros((LANES - rows, width), f32)
    return jnp.concatenate([tile, pad], axis=0).T


def pack_kernel(i_hbm, v_hbm, o_hbm, g_hbm, own_ref, other_ref, i_ref, v_ref, o_ref, g_ref, sems):
    copies = [
        pltpu.make_async_copy(src, dst, sems.at[k])
        for k, (src, dst) in enumerate(
            ((i_hbm, i_ref), (v_hbm, v_ref), (o_hbm, o_ref), (g_hbm, g_ref))
        )
    ]
    for copy in copies:
        copy.start()
    for copy in copies:
        copy.wait()
    tok = g_ref.shape[0]
    half = i_ref.shape[0] // 2
    core = lax.axis_index(CORE)
    for h, ref in ((core, own_ref), (1 - core, other_ref)):
        ref[:tok] = g_ref[...]
        for b in range(half // SUB):
            src = pl.ds(pl.multiple_of(2 * SUB * b + SUB * h, SUB), SUB)
            gated = (i_ref[src, :].astype(f32) * v_ref[src, :].astype(f32)).astype(bf16)
            ref[pl.ds(tok + SUB * b, SUB), :] = gated
            ref[pl.ds(tok + half + SUB * b, SUB), :] = o_ref[src, :]


def both_kernel(own_ref, other_ref, out_ref):
    core = lax.axis_index(CORE)
    out_ref[core] = own_ref[...]
    out_ref[1 - core] = other_ref[...]


def modes_kernel(d_ref, c_ref, od_ref, oc_ref):
    chan = lax.broadcasted_iota(jnp.int32, (d_ref.shape[1], LANES), 0)
    lane = lax.broadcasted_iota(jnp.int32, (d_ref.shape[1], LANES), 1)
    wanted = lane + SUB * (lane // SUB) + SUB * lax.axis_index(CORE)
    pick = jnp.where((chan == wanted) & (lane < d_ref.shape[1] // 2), 1.0, 0.0).astype(f32)
    for src, dst in ((d_ref, od_ref), (c_ref, oc_ref)):
        dst[...] = jnp.dot(
            src[...], pick, precision=lax.Precision.HIGHEST, preferred_element_type=f32
        )


def weight_rows(w_ref, core, block, count):
    blocks = w_ref.shape[0] // (2 * SUB * count)
    rows = []
    for b in range(blocks):
        start = 2 * SUB * (block * blocks + b) + SUB * core
        rows.append(w_ref[pl.ds(pl.multiple_of(start, SUB), SUB), :])
    return jnp.concatenate(rows, axis=0)


def back_kernel(w_ref, g_ref, out_ref):
    chan = 6 * SUB
    grads = g_ref[...]
    for j in range(w_ref.shape[0] // chan):
        part = lax.dot_general(
            w_ref[pl.ds(j * chan, chan), :],
            grads,
            (((1,), (1,)), ((), ())),
            preferred_element_type=f32,
        ).astype(bf16)
        for b in range(6):
            dst = j * chan + (b % 2) * 3 * SUB + (b // 2) * SUB
            out_ref[pl.ds(dst, SUB), :] = part[b * SUB : (b + 1) * SUB]


def split_kernel(p_ref, *outs):
    rows = p_ref.shape[0] // len(outs)
    for k, ref in enumerate(outs):
        block = lax.rem(lax.axis_index(ZL) + k, len(outs))
        ref[...] = p_ref[pl.ds(pl.multiple_of(block * rows, rows), rows), :]


def sum_kernel(p0, p1, p2, p3, own_ref, other_ref):
    half = own_ref.shape[0]
    core = lax.axis_index(CORE)
    for h, ref in ((core, own_ref), (1 - core, other_ref)):
        at = pl.ds(pl.multiple_of(h * half, half), half)
        total = p0[at, :].astype(f32)
        for p in (p1, p2, p3):
            total = total + p[at, :].astype(f32)
        ref[...] = total


def scan(src, y_ref, rate, coef, reverse):
    length = src.shape[0]

    def step(i, state):
        lo = length - 8 - i * 8 if reverse else i * 8
        at = pl.ds(pl.multiple_of(lo, 8), 8)
        block = src[at, :]
        rows = [None] * 8
        for t in range(8):
            u = 7 - t if reverse else t
            state = state * rate + block[u : u + 1, :]
            rows[u] = jnp.sum(state * coef, axis=0, keepdims=True)
        y_ref[at, :] = jnp.concatenate(rows, axis=0)
        return state

    return lax.fori_loop(0, length // 8, step, jnp.zeros_like(coef))


def heads(y_ref, out, state, rate, reverse):
    length = y_ref.shape[0]

    def step(i, state):
        lo = length - 8 - i * 8 if reverse else i * 8
        at = pl.ds(pl.multiple_of(lo, 8), 8)
        rows = [None] * 8
        for t in range(8):
            u = 7 - t if reverse else t
            state = state * rate
            rows[u] = jnp.sum(state, axis=0, keepdims=True)
        out[at, :] = y_ref[at, :] + jnp.concatenate(rows, axis=0)
        return state

    lax.fori_loop(0, length // 8, step, state)


def scan_forward_kernel(got_ref, d_ref, c_ref, y_ref, s_ref, gt):
    tok = got_ref.shape[2]
    half = (got_ref.shape[1] - tok) // 2
    for h in range(2):
        gt[pl.ds(h * tok, tok), :] = to_columns(got_ref[h, tok : tok + half].astype(f32))
    state = scan(gt, y_ref, jnp.exp(-d_ref[...]), c_ref[...], False)
    for m in range(s_ref.shape[0]):
        s_ref[m] = state


def heads_forward_kernel(s_ref, d_ref, c_ref, y_ref, got_ref, p_ref, f_ref, ft):
    tok = got_ref.shape[2]
    half = f_ref.shape[1]
    decay = d_ref[...]
    jump = jnp.exp(-decay * float(ft.shape[0]))
    state = jnp.zeros_like(decay)
    for m in range(s_ref.shape[0]):
        state = jnp.where(m < lax.axis_index(CHIP), state * jump + s_ref[m], state)
    heads(y_ref, ft, state * c_ref[...], jnp.exp(-decay), False)
    for h in range(2):
        at = pl.ds(h * tok, tok)
        filtered = ft[at, :].T[:half].astype(bf16)
        f_ref[h] = filtered
        product = (got_ref[h, tok + half :].astype(f32) * filtered.astype(f32)).astype(bf16)
        for q in range(p_ref.shape[0]):
            p_ref[q, :, at] = product


def scan_backward_kernel(own_ref, other_ref, got_ref, d_ref, c_ref, y_ref, s_ref, b_ref, bt):
    tok = got_ref.shape[2]
    half = own_ref.shape[0]
    core = lax.axis_index(CORE)
    b_ref[core] = own_ref[...]
    b_ref[1 - core] = other_ref[...]
    for h in range(2):
        outer = got_ref[h, tok + half :].astype(f32)
        bt[pl.ds(h * tok, tok), :] = to_columns((b_ref[h] * outer).astype(bf16).astype(f32))
    state = scan(bt, y_ref, jnp.exp(-d_ref[...]), c_ref[...], True)
    put_state(s_ref, state)


def put_state(ref, state):
    first = state.astype(bf16)
    ref[:, :LANES] = first
    ref[:, LANES:] = (state - first.astype(f32)).astype(bf16)


def get_state(ref):
    both = ref.astype(f32)
    return both[:, :LANES] + both[:, LANES:]


def weight_kernel(p_ref, got_ref, s_ref, out_ref):
    tok = got_ref.shape[2]
    n = out_ref.shape[0]
    rows = p_ref.shape[0] // n
    grads = got_ref[:, :tok, :].reshape(2 * tok, -1)
    for y in range(n):
        part = jnp.dot(p_ref[pl.ds(y * rows, rows), :], grads, preferred_element_type=f32)
        out_ref[y, :rows, :] = part.astype(bf16)
        out_ref[y, rows:, :] = s_ref[...]


def middle_kernel(t_ref, d_ref, out_ref):
    n = t_ref.shape[0]
    zs, rows = out_ref.shape[0], 2 * SUB
    length = 2.0 * t_ref.shape[2]
    decay = d_ref[...]
    y, zh = lax.axis_index(Y), lax.axis_index(ZH)
    jump = jnp.exp(-decay * (zs * length))
    later = jnp.zeros_like(decay)
    here = jnp.zeros_like(decay)
    for k in range(n - 1, -1, -1):
        state = get_state(t_ref[k, zs * rows :, :])
        later = jnp.where(k > y, later * jump + state, later)
        here = jnp.where(k == y, state, here)
    for z in range(zs):
        total = t_ref[0, pl.ds(z * rows, rows), :].astype(f32)
        for k in range(1, n):
            total = total + t_ref[k, pl.ds(z * rows, rows), :].astype(f32)
        out_ref[z, :rows, :] = total.astype(bf16)
        far = (zs - 1 + zh - z).astype(f32) * length
        near = jnp.maximum(zh - z - 1, 0).astype(f32) * length
        carry = jnp.exp(-decay * far) * later
        carry = jnp.where(zh > z, carry + jnp.exp(-decay * near) * here, carry)
        put_state(out_ref.at[z, rows:, :], carry)


def mixed_kernel(p_ref, w_ref, own_ref, other_ref, total):
    tok = own_ref.shape[1]
    total[...] = lax.dot_general(
        weight_rows(w_ref, lax.axis_index(CORE), 0, 1),
        p_ref[...],
        (((0,), (0,)), ((), ())),
        preferred_element_type=f32,
    )
    core = lax.axis_index(CORE)
    own_ref[...] = total[:, pl.ds(pl.multiple_of(core * tok, tok), tok)]
    other_ref[...] = total[:, pl.ds(pl.multiple_of((1 - core) * tok, tok), tok)]


def last_kernel(scale, t_ref, d_ref, c_ref, y_ref, f_ref, b_ref, own_ref, other_ref, bt):
    half, tok = f_ref.shape[1:]
    rows = 2 * SUB
    decay = d_ref[...]
    state = get_state(t_ref[0, rows:, :])
    for m in range(1, t_ref.shape[0]):
        state = state + get_state(t_ref[m, rows:, :])
    heads(y_ref, bt, state * c_ref[...], jnp.exp(-decay), True)
    core = lax.axis_index(CORE)
    for h, ref in ((core, own_ref), (1 - core, other_ref)):
        at = pl.ds(pl.multiple_of(h * tok, tok), tok)
        ref[:half] = bt[at, :].T[:half].astype(bf16).astype(f32)
        ref[half : 2 * half] = (b_ref[h] * f_ref[h].astype(f32)).astype(bf16).astype(f32)
        mine = pl.ds(pl.multiple_of(h * SUB, SUB), SUB)
        total = t_ref[0, mine, :].astype(f32)
        for m in range(1, t_ref.shape[0]):
            total = total + t_ref[m, mine, :].astype(f32)
        ref[2 * half :] = total * scale


def finish_kernel(m_ref, mr_ref, own_ref, other_ref, i_ref, v_ref, mixed_ref, go_ref, gi_ref, gv_ref, gw_ref):
    mixed_ref[...] = (m_ref[...] + mr_ref[...]).T.astype(bf16)
    half = i_ref.shape[0] // 2
    core = lax.axis_index(CORE)
    for h, ref in ((core, own_ref), (1 - core, other_ref)):
        for b in range(half // SUB):
            at = pl.ds(pl.multiple_of(2 * SUB * b + SUB * h, SUB), SUB)
            back = ref[pl.ds(SUB * b, SUB), :]
            go_ref[at, :] = ref[pl.ds(half + SUB * b, SUB), :].astype(bf16)
            gi_ref[at, :] = (back * v_ref[at, :].astype(f32)).astype(bf16)
            gv_ref[at, :] = (back * i_ref[at, :].astype(f32)).astype(bf16)
        gw_ref[pl.ds(pl.multiple_of(SUB * h, SUB), SUB), :] = ref[2 * half :]


def call(kernel, name, outs, args, scratch=(), cost=None):
    specs = [pl.BlockSpec(memory_space=pltpu.VMEM)] * len(args)
    return pl.pallas_call(
        kernel,
        out_shape=tuple(jax.ShapeDtypeStruct(s, t) for s, t in outs),
        in_specs=specs,
        out_specs=tuple([pl.BlockSpec(memory_space=pltpu.VMEM)] * len(outs)),
        scratch_shapes=[pltpu.VMEM(s, f32) for s in scratch],
        compiler_params=pltpu.CompilerParams(vmem_limit_bytes=24 * 2**20),
        cost_estimate=cost,
        name=name,
    )(*args)


def swap(x, axes):
    return lax.all_to_all(x, axes, 0, 0, tiled=True)


def spread(x, axis):
    n, rows, m = x.shape
    return swap(x.reshape(n * rows, m), axis)


def shift(x, axis, k):
    n = lax.axis_size(axis)
    return lax.ppermute(x, axis, [(i, (i + k) % n) for i in range(n)])


def other_core(x):
    return lax.ppermute(x, "core", [(0, 1), (1, 0)])


def shards(outer_gate, inner_gate, value_proj, residues, decays, out_weight, out_grad):
    chan, tok = outer_gate.shape
    half = chan // 2
    length = 2 * tok
    all_chan, cols = out_weight.shape
    modes = decays.shape[1]
    ny, nh, nx, nz = (lax.axis_size(axis) for axis in ("y", "zh", "x", "zl"))
    chips = ny * nh

    (part,) = call(back_kernel, "back", [((all_chan, tok), bf16)], (out_weight, out_grad))
    part = lax.psum_scatter(part, "x", scatter_dimension=0, tiled=True)

    packed = ((tok + chan, cols), bf16)
    vmem = pl.BlockSpec(memory_space=pltpu.VMEM)
    anywhere = pl.BlockSpec(memory_space=pl.ANY)
    own, other = pl.pallas_call(
        pack_kernel,
        out_shape=(jax.ShapeDtypeStruct(*packed),) * 2,
        in_specs=[anywhere] * 4,
        out_specs=(vmem,) * 2,
        scratch_shapes=[pltpu.VMEM((chan, tok), bf16)] * 3
        + [pltpu.VMEM((tok, cols), bf16), pltpu.SemaphoreType.DMA((4,))],
        name="pack",
    )(inner_gate, value_proj, outer_gate, out_grad)
    (got,) = call(
        both_kernel, "both", [((2, tok + chan, cols), bf16)], (own, other_core(other))
    )
    coef = residues * jnp.sqrt(-jnp.expm1(-2.0 * decays))
    small = ((modes, LANES), f32)
    decay, coef = call(modes_kernel, "modes", [small, small], (decays.T, coef.T))

    columns = ((length, LANES), f32)
    yf, states = call(
        scan_forward_kernel,
        "scan_forward",
        [columns, ((chips, modes, LANES), f32)],
        (got, decay, coef),
        scratch=[(length, LANES)],
    )
    states = swap(states, ("y", "zh"))
    product, filtered = call(
        heads_forward_kernel,
        "heads_forward",
        [((nz, half, length), bf16), ((2, half, tok), bf16)],
        (states, decay, coef, yf, got),
        scratch=[(length, LANES)],
    )
    product = spread(product, "zl")

    part, product = lax.optimization_barrier((part, product))
    own, *parts = call(split_kernel, "split", [((chan, tok), bf16)] * nz, (part,))
    own, other = call(
        sum_kernel,
        "sum",
        [((half, tok), f32)] * 2,
        (own, *(shift(part, "zl", k + 1) for k, part in enumerate(parts))),
    )
    product = spread(jnp.broadcast_to(product[None], (nx,) + product.shape), "x")
    yb, state, back_sum = call(
        scan_backward_kernel,
        "scan_backward",
        [columns, ((modes, 2 * LANES), bf16), ((2, half, tok), f32)],
        (own, other_core(other), got, decay, coef),
        scratch=[(length, LANES)],
    )

    (partial,) = call(
        weight_kernel,
        "weight",
        [((ny, nh * 2 * SUB + modes, cols), bf16)],
        (product, got, state),
    )
    partial = swap(partial, "y")
    (partial,) = call(
        middle_kernel, "middle", [((nh, 2 * SUB + modes, cols), bf16)], (partial, decay)
    )
    partial = swap(partial, "zh")
    mixed, mixed_other = call(
        mixed_kernel,
        "mixed",
        [((cols, tok), f32)] * 2,
        (product, out_weight),
        scratch=[(cols, length)],
    )
    mixed_other = other_core(mixed_other)
    scale = 1.0 / math.sqrt(length * chips)
    own, other = call(
        lambda *refs: last_kernel(scale, *refs),
        "last",
        [((chan + SUB, cols), f32)] * 2,
        (partial, decay, coef, yb, filtered, back_sum),
        scratch=[(length, LANES)],
    )
    return call(
        finish_kernel,
        "finish",
        [((tok, cols), bf16)] + [((chan, tok), bf16)] * 3 + [((2 * SUB, cols), f32)],
        (mixed, mixed_other, own, other_core(other), inner_gate, value_proj),
    )


def solution(mesh):
    fine = Mesh(mesh.devices.reshape(8, 3, 2, 4, 4), ("y", "zh", "core", "x", "zl"))
    seq, col = ("y", "zh", "core"), ("x", "zl")
    return jax.shard_map(
        shards,
        mesh=fine,
        in_specs=(
            P(col, seq),
            P(col, seq),
            P(col, seq),
            P(col, None),
            P(col, None),
            P(None, col),
            P(seq, col),
        ),
        out_specs=(P(seq, col), P(col, seq), P(col, seq), P(col, seq), P(seq, col)),
        check_vma=False,
    )
```

```python
import math

import jax
import jax.numpy as jnp
from jax import lax
from jax.experimental import pallas as pl
from jax.experimental.pallas import tpu as pltpu
from jax.sharding import Mesh
from jax.sharding import PartitionSpec as P

f32 = jnp.float32
bf16 = jnp.bfloat16
SUB = 32
LANES = 128
CORE, X, ZL, Y, ZH, CHIP = "core", "x", "zl", "y", "zh", ("y", "zh")


def to_columns(tile):
    rows, width = tile.shape
    pad = jnp.zeros((LANES - rows, width), f32)
    return jnp.concatenate([tile, pad], axis=0).T


def pack_kernel(i_hbm, v_hbm, o_hbm, g_hbm, own_ref, other_ref, i_ref, v_ref, o_ref, g_ref, sems):
    fetch(sems, (i_hbm, i_ref), (v_hbm, v_ref), (o_hbm, o_ref), (g_hbm, g_ref))
    tok = g_ref.shape[0]
    half = i_ref.shape[0] // 2
    core = lax.axis_index(CORE)
    for h, ref in ((core, own_ref), (1 - core, other_ref)):
        ref[:tok] = g_ref[...]
        for b in range(half // SUB):
            src = pl.ds(pl.multiple_of(2 * SUB * b + SUB * h, SUB), SUB)
            gated = (i_ref[src, :].astype(f32) * v_ref[src, :].astype(f32)).astype(bf16)
            ref[pl.ds(tok + SUB * b, SUB), :] = gated
            ref[pl.ds(tok + half + SUB * b, SUB), :] = o_ref[src, :]


def fetch(sems, *pairs):
    copies = [pltpu.make_async_copy(src, dst, sems.at[k]) for k, (src, dst) in enumerate(pairs)]
    for copy in copies:
        copy.start()
    for copy in copies:
        copy.wait()


def both_kernel(own_hbm, other_hbm, out_ref, sems):
    core = lax.axis_index(CORE)
    fetch(sems, (own_hbm, out_ref.at[core]), (other_hbm, out_ref.at[1 - core]))


def modes_kernel(d_ref, c_ref, od_ref, oc_ref):
    chan = lax.broadcasted_iota(jnp.int32, (d_ref.shape[1], LANES), 0)
    lane = lax.broadcasted_iota(jnp.int32, (d_ref.shape[1], LANES), 1)
    wanted = lane + SUB * (lane // SUB) + SUB * lax.axis_index(CORE)
    pick = jnp.where((chan == wanted) & (lane < d_ref.shape[1] // 2), 1.0, 0.0).astype(f32)
    for src, dst in ((d_ref, od_ref), (c_ref, oc_ref)):
        dst[...] = jnp.dot(
            src[...], pick, precision=lax.Precision.HIGHEST, preferred_element_type=f32
        )


def weight_rows(w_ref, core, block, count):
    blocks = w_ref.shape[0] // (2 * SUB * count)
    rows = []
    for b in range(blocks):
        start = 2 * SUB * (block * blocks + b) + SUB * core
        rows.append(w_ref[pl.ds(pl.multiple_of(start, SUB), SUB), :])
    return jnp.concatenate(rows, axis=0)


def back_kernel(w_ref, g_ref, *outs):
    chan = 6 * SUB
    n = len(outs)
    rows = w_ref.shape[0] // n
    grads = g_ref[...]
    for k, ref in enumerate(outs):
        block = lax.rem(lax.axis_index(X) + k, n)
        for j in range(rows // chan):
            at = pl.ds(pl.multiple_of(block * rows + j * chan, chan), chan)
            part = lax.dot_general(
                w_ref[at, :], grads, (((1,), (1,)), ((), ())), preferred_element_type=f32
            ).astype(bf16)
            for b in range(6):
                dst = j * chan + (b % 2) * 3 * SUB + (b // 2) * SUB
                ref[pl.ds(dst, SUB), :] = part[b * SUB : (b + 1) * SUB]


def split_kernel(p0, p1, p2, p3, *outs):
    rows = p0.shape[0] // len(outs)
    for k, ref in enumerate(outs):
        block = lax.rem(lax.axis_index(ZL) + k, len(outs))
        at = pl.ds(pl.multiple_of(block * rows, rows), rows)
        total = p0[at, :].astype(f32)
        for p in (p1, p2, p3):
            total = total + p[at, :].astype(f32)
        ref[...] = total.astype(bf16)


def sum_kernel(p0, p1, p2, p3, own_ref, other_ref):
    half = own_ref.shape[0]
    core = lax.axis_index(CORE)
    for h, ref in ((core, own_ref), (1 - core, other_ref)):
        at = pl.ds(pl.multiple_of(h * half, half), half)
        total = p0[at, :].astype(f32)
        for p in (p1, p2, p3):
            total = total + p[at, :].astype(f32)
        ref[...] = total


def scan(src, y_ref, rate, coef, reverse):
    length = src.shape[0]

    def step(i, state):
        lo = length - 8 - i * 8 if reverse else i * 8
        at = pl.ds(pl.multiple_of(lo, 8), 8)
        block = src[at, :]
        rows = [None] * 8
        for t in range(8):
            u = 7 - t if reverse else t
            state = state * rate + block[u : u + 1, :]
            rows[u] = jnp.sum(state * coef, axis=0, keepdims=True)
        y_ref[at, :] = jnp.concatenate(rows, axis=0)
        return state

    return lax.fori_loop(0, length // 8, step, jnp.zeros_like(coef))


def heads(y_ref, out, state, rate, reverse):
    length = y_ref.shape[0]

    def step(i, state):
        lo = length - 8 - i * 8 if reverse else i * 8
        at = pl.ds(pl.multiple_of(lo, 8), 8)
        rows = [None] * 8
        for t in range(8):
            u = 7 - t if reverse else t
            state = state * rate
            rows[u] = jnp.sum(state, axis=0, keepdims=True)
        out[at, :] = y_ref[at, :] + jnp.concatenate(rows, axis=0)
        return state

    lax.fori_loop(0, length // 8, step, state)


def scan_forward_kernel(got_ref, d_ref, c_ref, y_ref, s_ref, gt):
    tok = got_ref.shape[2]
    half = (got_ref.shape[1] - tok) // 2
    for h in range(2):
        gt[pl.ds(h * tok, tok), :] = to_columns(got_ref[h, tok : tok + half].astype(f32))
    state = scan(gt, y_ref, jnp.exp(-d_ref[...]), c_ref[...], False)
    for m in range(s_ref.shape[0]):
        s_ref[m] = state


def heads_forward_kernel(s_ref, d_ref, c_ref, y_ref, got_ref, p_ref, f_ref, ft):
    tok = got_ref.shape[2]
    half = f_ref.shape[1]
    decay = d_ref[...]
    jump = jnp.exp(-decay * float(ft.shape[0]))
    state = jnp.zeros_like(decay)
    for m in range(s_ref.shape[0]):
        state = jnp.where(m < lax.axis_index(CHIP), state * jump + s_ref[m], state)
    heads(y_ref, ft, state * c_ref[...], jnp.exp(-decay), False)
    for h in range(2):
        at = pl.ds(h * tok, tok)
        filtered = ft[at, :].T[:half].astype(bf16)
        f_ref[h] = filtered
        product = (got_ref[h, tok + half :].astype(f32) * filtered.astype(f32)).astype(bf16)
        for q in range(p_ref.shape[0]):
            p_ref[q, :, at] = product


def scan_backward_kernel(own_ref, other_ref, f_ref, got_ref, d_ref, c_ref, y_ref, s_ref, go_ref, gx_ref, bt):
    tok = got_ref.shape[2]
    half = own_ref.shape[0]
    core = lax.axis_index(CORE)
    for h, ref, out in ((core, own_ref, go_ref), (1 - core, other_ref, gx_ref)):
        total = ref[...]
        out[...] = (total * f_ref[h].astype(f32)).astype(bf16)
        outer = got_ref[h, tok + half :].astype(f32)
        at = pl.ds(pl.multiple_of(h * tok, tok), tok)
        bt[at, :] = to_columns((total * outer).astype(bf16).astype(f32))
    state = scan(bt, y_ref, jnp.exp(-d_ref[...]), c_ref[...], True)
    put_state(s_ref, state)


def put_state(ref, state):
    first = state.astype(bf16)
    ref[:, :LANES] = first
    ref[:, LANES:] = (state - first.astype(f32)).astype(bf16)


def get_state(ref):
    both = ref.astype(f32)
    return both[:, :LANES] + both[:, LANES:]


def weight_kernel(p_ref, got_ref, s_ref, out_ref):
    tok = got_ref.shape[2]
    n = out_ref.shape[0]
    rows = p_ref.shape[0] // n
    grads = got_ref[:, :tok, :].reshape(2 * tok, -1)
    for y in range(n):
        part = jnp.dot(p_ref[pl.ds(y * rows, rows), :], grads, preferred_element_type=f32)
        out_ref[y, :rows, :] = part.astype(bf16)
        out_ref[y, rows:, :] = s_ref[...]


def middle_kernel(t_ref, d_ref, out_ref):
    n = t_ref.shape[0]
    zs, rows = out_ref.shape[0], 2 * SUB
    length = 2.0 * t_ref.shape[2]
    decay = d_ref[...]
    y, zh = lax.axis_index(Y), lax.axis_index(ZH)
    jump = jnp.exp(-decay * (zs * length))
    later = jnp.zeros_like(decay)
    here = jnp.zeros_like(decay)
    for k in range(n - 1, -1, -1):
        state = get_state(t_ref[k, zs * rows :, :])
        later = jnp.where(k > y, later * jump + state, later)
        here = jnp.where(k == y, state, here)
    for z in range(zs):
        total = t_ref[0, pl.ds(z * rows, rows), :].astype(f32)
        for k in range(1, n):
            total = total + t_ref[k, pl.ds(z * rows, rows), :].astype(f32)
        out_ref[z, :rows, :] = total.astype(bf16)
        far = (zs - 1 + zh - z).astype(f32) * length
        near = jnp.maximum(zh - z - 1, 0).astype(f32) * length
        carry = jnp.exp(-decay * far) * later
        carry = jnp.where(zh > z, carry + jnp.exp(-decay * near) * here, carry)
        put_state(out_ref.at[z, rows:, :], carry)


def mixed_kernel(p_ref, w_ref, own_ref, other_ref, total):
    tok = own_ref.shape[1]
    total[...] = lax.dot_general(
        weight_rows(w_ref, lax.axis_index(CORE), 0, 1),
        p_ref[...],
        (((0,), (0,)), ((), ())),
        preferred_element_type=f32,
    )
    core = lax.axis_index(CORE)
    own_ref[...] = total[:, pl.ds(pl.multiple_of(core * tok, tok), tok)]
    other_ref[...] = total[:, pl.ds(pl.multiple_of((1 - core) * tok, tok), tok)]


def last_kernel(scale, d_ref, c_ref, t_hbm, y_hbm, own_ref, other_ref, t_ref, y_ref, bt, sems):
    fetch(sems, (t_hbm, t_ref), (y_hbm, y_ref))
    rows = 2 * SUB
    tok = y_ref.shape[0] // 2
    half = own_ref.shape[0] - SUB
    state = get_state(t_ref[0, rows:, :])
    for m in range(1, t_ref.shape[0]):
        state = state + get_state(t_ref[m, rows:, :])
    core = lax.axis_index(CORE)
    for h, ref in ((core, own_ref), (1 - core, other_ref)):
        mine = pl.ds(pl.multiple_of(h * SUB, SUB), SUB)
        total = t_ref[0, mine, :].astype(f32)
        for m in range(1, t_ref.shape[0]):
            total = total + t_ref[m, mine, :].astype(f32)
        ref[half:] = total * scale
    heads(y_ref, bt, state * c_ref[...], jnp.exp(-d_ref[...]), True)
    for h, ref in ((core, own_ref), (1 - core, other_ref)):
        at = pl.ds(pl.multiple_of(h * tok, tok), tok)
        ref[:half] = bt[at, :].T[:half].astype(bf16).astype(f32)


def halves(core, own_ref, other_ref, count):
    for h, ref in ((core, own_ref), (1 - core, other_ref)):
        for b in range(count):
            at = pl.ds(pl.multiple_of(2 * SUB * b + SUB * h, SUB), SUB)
            yield at, ref, pl.ds(SUB * b, SUB)


def finish_kernel(m_ref, mr_ref, own_ref, other_ref, mixed_ref, go_ref):
    mixed_ref[...] = (m_ref[...] + mr_ref[...]).T.astype(bf16)
    for at, ref, src in halves(lax.axis_index(CORE), own_ref, other_ref, own_ref.shape[0] // SUB):
        go_ref[at, :] = ref[src, :]


def end_kernel(own_hbm, other_hbm, i_hbm, v_hbm, gi_ref, gv_ref, gw_ref, own_ref, other_ref, i_ref, v_ref, sems):
    fetch(sems, (own_hbm, own_ref), (other_hbm, other_ref), (i_hbm, i_ref), (v_hbm, v_ref))
    half = i_ref.shape[0] // 2
    core = lax.axis_index(CORE)
    for at, ref, src in halves(core, own_ref, other_ref, half // SUB):
        back = ref[src, :]
        gi_ref[at, :] = (back * v_ref[at, :].astype(f32)).astype(bf16)
        gv_ref[at, :] = (back * i_ref[at, :].astype(f32)).astype(bf16)
    for h, ref in ((core, own_ref), (1 - core, other_ref)):
        gw_ref[pl.ds(pl.multiple_of(SUB * h, SUB), SUB), :] = ref[half:]


def call(kernel, name, outs, args, scratch=(), cost=None, remote=0, limit=24):
    specs = [pl.BlockSpec(memory_space=pltpu.VMEM)] * (len(args) - remote)
    specs += [pl.BlockSpec(memory_space=pl.ANY)] * remote
    return pl.pallas_call(
        kernel,
        out_shape=tuple(jax.ShapeDtypeStruct(s, t) for s, t in outs),
        in_specs=specs,
        out_specs=tuple([pl.BlockSpec(memory_space=pltpu.VMEM)] * len(outs)),
        scratch_shapes=[pltpu.VMEM(s, t) for s, t in scratch]
        + ([pltpu.SemaphoreType.DMA((remote,))] if remote else []),
        compiler_params=None if limit is None else pltpu.CompilerParams(vmem_limit_bytes=limit * 2**20),
        cost_estimate=cost,
        name=name,
    )(*args)


LONG = pl.CostEstimate(flops=10**11, bytes_accessed=0, transcendentals=0)


def swap(x, axes):
    return lax.all_to_all(x, axes, 0, 0, tiled=True)


def spread(x, axis):
    n, rows, m = x.shape
    return swap(x.reshape(n * rows, m), axis)


def shift(x, axis, k):
    n = lax.axis_size(axis)
    return lax.ppermute(x, axis, [(i, (i + k) % n) for i in range(n)])


def other_core(x):
    return lax.ppermute(x, "core", [(0, 1), (1, 0)])


def shards(outer_gate, inner_gate, value_proj, residues, decays, out_weight, out_grad):
    chan, tok = outer_gate.shape
    half = chan // 2
    length = 2 * tok
    all_chan, cols = out_weight.shape
    modes = decays.shape[1]
    ny, nh, nx, nz = (lax.axis_size(axis) for axis in ("y", "zh", "x", "zl"))
    chips = ny * nh

    packed = ((tok + chan, cols), bf16)
    gate = ((chan, tok), bf16)
    own, other = call(
        pack_kernel,
        "pack",
        [packed] * 2,
        (inner_gate, value_proj, outer_gate, out_grad),
        scratch=[gate] * 3 + [((tok, cols), bf16)],
        remote=4,
        limit=None,
    )
    (got,) = call(
        both_kernel, "both", [((2, tok + chan, cols), bf16)], (own, other_core(other)), remote=2
    )
    coef = residues * jnp.sqrt(-jnp.expm1(-2.0 * decays))
    small = ((modes, LANES), f32)
    decay, coef = call(modes_kernel, "modes", [small, small], (decays.T, coef.T))

    columns = ((length, LANES), f32)
    yf, states = call(
        scan_forward_kernel,
        "scan_forward",
        [columns, ((chips, modes, LANES), f32)],
        (got, decay, coef),
        scratch=[columns],
    )
    states = swap(states, ("y", "zh"))
    product, filtered = call(
        heads_forward_kernel,
        "heads_forward",
        [((nz, half, length), bf16), ((2, half, tok), bf16)],
        (states, decay, coef, yf, got),
        scratch=[columns],
    )

    parts = call(
        back_kernel, "back", [((all_chan // nx, tok), bf16)] * nx, (out_weight, out_grad)
    )
    product, *parts = lax.optimization_barrier((product, *parts))
    product = spread(product, "zl")
    parts = [parts[0]] + [shift(part, "x", k) for k, part in enumerate(parts) if k]

    own, *parts = call(split_kernel, "split", [gate] * nz, parts, cost=LONG)
    own, other = call(
        sum_kernel,
        "sum",
        [((half, tok), f32)] * 2,
        (own, *(shift(part, "zl", k + 1) for k, part in enumerate(parts))),
    )
    product = spread(jnp.broadcast_to(product[None], (nx,) + product.shape), "x")
    yb, state, grad_outer, grad_outer_other = call(
        scan_backward_kernel,
        "scan_backward",
        [columns, ((modes, 2 * LANES), bf16)] + [((half, tok), bf16)] * 2,
        (own, other_core(other), filtered, got, decay, coef),
        scratch=[columns],
    )

    (partial,) = call(
        weight_kernel,
        "weight",
        [((ny, nh * 2 * SUB + modes, cols), bf16)],
        (product, got, state),
    )
    partial = swap(partial, "y")
    (partial,) = call(
        middle_kernel, "middle", [((nh, 2 * SUB + modes, cols), bf16)], (partial, decay)
    )
    partial = swap(partial, "zh")
    mixed, mixed_other = call(
        mixed_kernel,
        "mixed",
        [((cols, tok), f32)] * 2,
        (product, out_weight),
        scratch=[((cols, length), f32)],
    )
    mixed, grad_outer = call(
        finish_kernel,
        "finish",
        [((tok, cols), bf16), gate],
        (mixed, other_core(mixed_other), grad_outer, other_core(grad_outer_other)),
    )
    mixed, grad_outer, partial = lax.optimization_barrier((mixed, grad_outer, partial))
    scale = 1.0 / math.sqrt(length * chips)
    late = ((half + SUB, cols), f32)
    own, other = call(
        lambda *refs: last_kernel(scale, *refs),
        "last",
        [late] * 2,
        (decay, coef, partial.reshape(nh, 2 * SUB + modes, cols), yb),
        scratch=[((nh, 2 * SUB + modes, cols), bf16), columns, columns],
        remote=2,
    )
    grad_inner, grad_value, grad_weight = call(
        end_kernel,
        "end",
        [gate, gate, ((2 * SUB, cols), f32)],
        (own, other_core(other), inner_gate, value_proj),
        scratch=[late, late, gate, gate],
        remote=4,
    )
    return (mixed, grad_outer, grad_inner, grad_value, grad_weight)


def solution(mesh):
    fine = Mesh(mesh.devices.reshape(8, 3, 2, 4, 4), ("y", "zh", "core", "x", "zl"))
    seq, col = ("y", "zh", "core"), ("x", "zl")
    return jax.shard_map(
        shards,
        mesh=fine,
        in_specs=(
            P(col, seq),
            P(col, seq),
            P(col, seq),
            P(col, None),
            P(col, None),
            P(None, col),
            P(seq, col),
        ),
        out_specs=(P(seq, col), P(col, seq), P(col, seq), P(col, seq), P(seq, col)),
        check_vma=False,
    )
```

```python
import math

import jax
import jax.numpy as jnp
from jax import lax
from jax.experimental import pallas as pl
from jax.experimental.pallas import tpu as pltpu
from jax.sharding import Mesh
from jax.sharding import PartitionSpec as P

f32 = jnp.float32
bf16 = jnp.bfloat16
SUB = 32
LANES = 128
CORE, X, ZL, Y, ZH, CHIP = "core", "x", "zl", "y", "zh", ("y", "zh")


def to_columns(tile):
    rows, width = tile.shape
    pad = jnp.zeros((LANES - rows, width), f32)
    return jnp.concatenate([tile, pad], axis=0).T


def pack_kernel(i_hbm, v_hbm, o_hbm, g_hbm, own_ref, other_ref, i_ref, v_ref, o_ref, g_ref, sems):
    fetch(sems, (i_hbm, i_ref), (v_hbm, v_ref), (o_hbm, o_ref), (g_hbm, g_ref))
    tok = g_ref.shape[0]
    half = i_ref.shape[0] // 2
    core = lax.axis_index(CORE)
    for h, ref in ((core, own_ref), (1 - core, other_ref)):
        ref[:tok] = g_ref[...]
        for b in range(half // SUB):
            src = pl.ds(pl.multiple_of(2 * SUB * b + SUB * h, SUB), SUB)
            gated = (i_ref[src, :].astype(f32) * v_ref[src, :].astype(f32)).astype(bf16)
            ref[pl.ds(tok + SUB * b, SUB), :] = gated
            ref[pl.ds(tok + half + SUB * b, SUB), :] = o_ref[src, :]


def fetch(sems, *pairs):
    copies = [pltpu.make_async_copy(src, dst, sems.at[k]) for k, (src, dst) in enumerate(pairs)]
    for copy in copies:
        copy.start()
    for copy in copies:
        copy.wait()


def both_kernel(own_hbm, other_hbm, out_ref, sems):
    core = lax.axis_index(CORE)
    fetch(sems, (own_hbm, out_ref.at[core]), (other_hbm, out_ref.at[1 - core]))


def modes_kernel(d_ref, c_ref, od_ref, oc_ref):
    chan = lax.broadcasted_iota(jnp.int32, (d_ref.shape[1], LANES), 0)
    lane = lax.broadcasted_iota(jnp.int32, (d_ref.shape[1], LANES), 1)
    wanted = lane + SUB * (lane // SUB) + SUB * lax.axis_index(CORE)
    pick = jnp.where((chan == wanted) & (lane < d_ref.shape[1] // 2), 1.0, 0.0).astype(f32)
    for src, dst in ((d_ref, od_ref), (c_ref, oc_ref)):
        dst[...] = jnp.dot(
            src[...], pick, precision=lax.Precision.HIGHEST, preferred_element_type=f32
        )


def weight_rows(w_ref, core, block, count):
    blocks = w_ref.shape[0] // (2 * SUB * count)
    rows = []
    for b in range(blocks):
        start = 2 * SUB * (block * blocks + b) + SUB * core
        rows.append(w_ref[pl.ds(pl.multiple_of(start, SUB), SUB), :])
    return jnp.concatenate(rows, axis=0)


def back_kernel(w_ref, g_ref, *outs):
    chan = 6 * SUB
    n = len(outs)
    rows = w_ref.shape[0] // n
    grads = g_ref[...]
    for k, ref in enumerate(outs):
        block = lax.rem(lax.axis_index(X) + k, n)
        for j in range(rows // chan):
            at = pl.ds(pl.multiple_of(block * rows + j * chan, chan), chan)
            part = lax.dot_general(
                w_ref[at, :], grads, (((1,), (1,)), ((), ())), preferred_element_type=f32
            ).astype(bf16)
            for b in range(6):
                dst = j * chan + (b % 2) * 3 * SUB + (b // 2) * SUB
                ref[pl.ds(dst, SUB), :] = part[b * SUB : (b + 1) * SUB]


def split_kernel(p0, p1, p2, p3, *outs):
    rows = p0.shape[0] // len(outs)
    for k, ref in enumerate(outs):
        block = lax.rem(lax.axis_index(ZL) + k, len(outs))
        at = pl.ds(pl.multiple_of(block * rows, rows), rows)
        total = p0[at, :].astype(f32)
        for p in (p1, p2, p3):
            total = total + p[at, :].astype(f32)
        ref[...] = total.astype(bf16)


def sum_kernel(p0, p1, p2, p3, own_ref, other_ref):
    half = own_ref.shape[0]
    core = lax.axis_index(CORE)
    for h, ref in ((core, own_ref), (1 - core, other_ref)):
        at = pl.ds(pl.multiple_of(h * half, half), half)
        total = p0[at, :].astype(f32)
        for p in (p1, p2, p3):
            total = total + p[at, :].astype(f32)
        ref[...] = total


def scan(src, y_ref, rate, coef, reverse):
    length = src.shape[0]

    def step(i, state):
        lo = length - 8 - i * 8 if reverse else i * 8
        at = pl.ds(pl.multiple_of(lo, 8), 8)
        block = src[at, :]
        rows = [None] * 8
        for t in range(8):
            u = 7 - t if reverse else t
            state = state * rate + block[u : u + 1, :]
            rows[u] = jnp.sum(state * coef, axis=0, keepdims=True)
        y_ref[at, :] = jnp.concatenate(rows, axis=0)
        return state

    return lax.fori_loop(0, length // 8, step, jnp.zeros_like(coef))


def heads(y_ref, out, state, rate, reverse):
    length = y_ref.shape[0]

    def step(i, state):
        lo = length - 8 - i * 8 if reverse else i * 8
        at = pl.ds(pl.multiple_of(lo, 8), 8)
        rows = [None] * 8
        for t in range(8):
            u = 7 - t if reverse else t
            state = state * rate
            rows[u] = jnp.sum(state, axis=0, keepdims=True)
        out[at, :] = y_ref[at, :] + jnp.concatenate(rows, axis=0)
        return state

    lax.fori_loop(0, length // 8, step, state)


def scan_forward_kernel(d_ref, c_ref, own_hbm, other_hbm, y_ref, s_ref, own_ref, other_ref, gt, sems):
    half, tok = own_ref.shape
    gated = pl.ds(tok, half)
    fetch(sems, (own_hbm.at[gated], own_ref), (other_hbm.at[gated], other_ref))
    core = lax.axis_index(CORE)
    for h, ref in ((core, own_ref), (1 - core, other_ref)):
        at = pl.ds(pl.multiple_of(h * tok, tok), tok)
        gt[at, :] = to_columns(ref[...].astype(f32))
    state = scan(gt, y_ref, jnp.exp(-d_ref[...]), c_ref[...], False)
    for m in range(s_ref.shape[0]):
        s_ref[m] = state


def heads_forward_kernel(s_ref, d_ref, c_ref, y_ref, got_ref, p_ref, f_ref, ft):
    tok = got_ref.shape[2]
    half = f_ref.shape[1]
    decay = d_ref[...]
    jump = jnp.exp(-decay * float(ft.shape[0]))
    state = jnp.zeros_like(decay)
    for m in range(s_ref.shape[0]):
        state = jnp.where(m < lax.axis_index(CHIP), state * jump + s_ref[m], state)
    heads(y_ref, ft, state * c_ref[...], jnp.exp(-decay), False)
    for h in range(2):
        at = pl.ds(h * tok, tok)
        filtered = ft[at, :].T[:half].astype(bf16)
        f_ref[h] = filtered
        product = (got_ref[h, tok + half :].astype(f32) * filtered.astype(f32)).astype(bf16)
        for q in range(p_ref.shape[0]):
            p_ref[q, :, at] = product


def scan_backward_kernel(own_ref, other_ref, f_ref, got_ref, d_ref, c_ref, y_ref, s_ref, go_ref, gx_ref, bt):
    tok = got_ref.shape[2]
    half = own_ref.shape[0]
    core = lax.axis_index(CORE)
    for h, ref, out in ((core, own_ref, go_ref), (1 - core, other_ref, gx_ref)):
        total = ref[...]
        out[...] = (total * f_ref[h].astype(f32)).astype(bf16)
        outer = got_ref[h, tok + half :].astype(f32)
        at = pl.ds(pl.multiple_of(h * tok, tok), tok)
        bt[at, :] = to_columns((total * outer).astype(bf16).astype(f32))
    state = scan(bt, y_ref, jnp.exp(-d_ref[...]), c_ref[...], True)
    put_state(s_ref, state)


def put_state(ref, state):
    first = state.astype(bf16)
    ref[:, :LANES] = first
    ref[:, LANES:] = (state - first.astype(f32)).astype(bf16)


def get_state(ref):
    both = ref.astype(f32)
    return both[:, :LANES] + both[:, LANES:]


def weight_kernel(p_ref, got_ref, s_ref, out_hbm, out_ref, sems):
    tok = got_ref.shape[2]
    n = out_ref.shape[0]
    rows = p_ref.shape[0] // n
    grads = got_ref[:, :tok, :].reshape(2 * tok, -1)
    copies = []
    for y in range(n):
        part = jnp.dot(p_ref[pl.ds(y * rows, rows), :], grads, preferred_element_type=f32)
        out_ref[y, :rows, :] = part.astype(bf16)
        out_ref[y, rows:, :] = s_ref[...]
        copies.append(pltpu.make_async_copy(out_ref.at[y], out_hbm.at[y], sems.at[y]))
        copies[-1].start()
    for copy in copies:
        copy.wait()


def middle_kernel(t_ref, d_ref, out_ref):
    n = t_ref.shape[0]
    zs, rows = out_ref.shape[0], 2 * SUB
    length = 2.0 * t_ref.shape[2]
    decay = d_ref[...]
    y, zh = lax.axis_index(Y), lax.axis_index(ZH)
    jump = jnp.exp(-decay * (zs * length))
    later = jnp.zeros_like(decay)
    here = jnp.zeros_like(decay)
    for k in range(n - 1, -1, -1):
        state = get_state(t_ref[k, zs * rows :, :])
        later = jnp.where(k > y, later * jump + state, later)
        here = jnp.where(k == y, state, here)
    for z in range(zs):
        total = t_ref[0, pl.ds(z * rows, rows), :].astype(f32)
        for k in range(1, n):
            total = total + t_ref[k, pl.ds(z * rows, rows), :].astype(f32)
        out_ref[z, :rows, :] = total.astype(bf16)
        far = (zs - 1 + zh - z).astype(f32) * length
        near = jnp.maximum(zh - z - 1, 0).astype(f32) * length
        carry = jnp.exp(-decay * far) * later
        carry = jnp.where(zh > z, carry + jnp.exp(-decay * near) * here, carry)
        put_state(out_ref.at[z, rows:, :], carry)


def mixed_kernel(p_ref, w_ref, own_ref, other_ref, total):
    tok = own_ref.shape[1]
    total[...] = lax.dot_general(
        weight_rows(w_ref, lax.axis_index(CORE), 0, 1),
        p_ref[...],
        (((0,), (0,)), ((), ())),
        preferred_element_type=f32,
    )
    core = lax.axis_index(CORE)
    own_ref[...] = total[:, pl.ds(pl.multiple_of(core * tok, tok), tok)]
    other_ref[...] = total[:, pl.ds(pl.multiple_of((1 - core) * tok, tok), tok)]


def last_kernel(scale, d_ref, c_ref, t_hbm, y_hbm, own_ref, other_ref, t_ref, y_ref, bt, sems):
    fetch(sems, (t_hbm, t_ref), (y_hbm, y_ref))
    rows = 2 * SUB
    tok = y_ref.shape[0] // 2
    half = own_ref.shape[0] - SUB
    state = get_state(t_ref[0, rows:, :])
    for m in range(1, t_ref.shape[0]):
        state = state + get_state(t_ref[m, rows:, :])
    core = lax.axis_index(CORE)
    for h, ref in ((core, own_ref), (1 - core, other_ref)):
        mine = pl.ds(pl.multiple_of(h * SUB, SUB), SUB)
        total = t_ref[0, mine, :].astype(f32)
        for m in range(1, t_ref.shape[0]):
            total = total + t_ref[m, mine, :].astype(f32)
        ref[half:] = total * scale
    heads(y_ref, bt, state * c_ref[...], jnp.exp(-d_ref[...]), True)
    for h, ref in ((core, own_ref), (1 - core, other_ref)):
        at = pl.ds(pl.multiple_of(h * tok, tok), tok)
        ref[:half] = bt[at, :].T[:half].astype(bf16).astype(f32)


def halves(core, own_ref, other_ref, count):
    for h, ref in ((core, own_ref), (1 - core, other_ref)):
        for b in range(count):
            at = pl.ds(pl.multiple_of(2 * SUB * b + SUB * h, SUB), SUB)
            yield at, ref, pl.ds(SUB * b, SUB)


def finish_kernel(m_ref, mr_ref, own_ref, other_ref, mixed_ref, go_ref):
    mixed_ref[...] = (m_ref[...] + mr_ref[...]).T.astype(bf16)
    for at, ref, src in halves(lax.axis_index(CORE), own_ref, other_ref, own_ref.shape[0] // SUB):
        go_ref[at, :] = ref[src, :]


def end_kernel(own_hbm, other_hbm, i_hbm, v_hbm, gi_ref, gv_ref, gw_ref, own_ref, other_ref, i_ref, v_ref, sems):
    fetch(sems, (own_hbm, own_ref), (other_hbm, other_ref), (i_hbm, i_ref), (v_hbm, v_ref))
    half = i_ref.shape[0] // 2
    core = lax.axis_index(CORE)
    for at, ref, src in halves(core, own_ref, other_ref, half // SUB):
        back = ref[src, :]
        gi_ref[at, :] = (back * v_ref[at, :].astype(f32)).astype(bf16)
        gv_ref[at, :] = (back * i_ref[at, :].astype(f32)).astype(bf16)
    for h, ref in ((core, own_ref), (1 - core, other_ref)):
        gw_ref[pl.ds(pl.multiple_of(SUB * h, SUB), SUB), :] = ref[half:]


def call(kernel, name, outs, args, scratch=(), cost=None, remote=0, limit=24):
    specs = [pl.BlockSpec(memory_space=pltpu.VMEM)] * (len(args) - remote)
    specs += [pl.BlockSpec(memory_space=pl.ANY)] * remote
    return pl.pallas_call(
        kernel,
        out_shape=tuple(jax.ShapeDtypeStruct(s, t) for s, t in outs),
        in_specs=specs,
        out_specs=tuple([pl.BlockSpec(memory_space=pltpu.VMEM)] * len(outs)),
        scratch_shapes=[pltpu.VMEM(s, t) for s, t in scratch]
        + ([pltpu.SemaphoreType.DMA((remote,))] if remote else []),
        compiler_params=None if limit is None else pltpu.CompilerParams(vmem_limit_bytes=limit * 2**20),
        cost_estimate=cost,
        name=name,
    )(*args)


LONG = pl.CostEstimate(flops=10**11, bytes_accessed=0, transcendentals=0)


def swap(x, axes):
    return lax.all_to_all(x, axes, 0, 0, tiled=True)


def spread(x, axis):
    n, rows, m = x.shape
    return swap(x.reshape(n * rows, m), axis)


def shift(x, axis, k):
    n = lax.axis_size(axis)
    return lax.ppermute(x, axis, [(i, (i + k) % n) for i in range(n)])


def other_core(x):
    return lax.ppermute(x, "core", [(0, 1), (1, 0)])


def shards(outer_gate, inner_gate, value_proj, residues, decays, out_weight, out_grad):
    chan, tok = outer_gate.shape
    half = chan // 2
    length = 2 * tok
    all_chan, cols = out_weight.shape
    modes = decays.shape[1]
    ny, nh, nx, nz = (lax.axis_size(axis) for axis in ("y", "zh", "x", "zl"))
    chips = ny * nh

    packed = ((tok + chan, cols), bf16)
    gate = ((chan, tok), bf16)
    own, other = call(
        pack_kernel,
        "pack",
        [packed] * 2,
        (inner_gate, value_proj, outer_gate, out_grad),
        scratch=[gate] * 3 + [((tok, cols), bf16)],
        remote=4,
        limit=None,
    )
    other = other_core(other)
    coef = residues * jnp.sqrt(-jnp.expm1(-2.0 * decays))
    small = ((modes, LANES), f32)
    decay, coef = call(modes_kernel, "modes", [small, small], (decays.T, coef.T))

    columns = ((length, LANES), f32)
    yf, states = call(
        scan_forward_kernel,
        "scan_forward",
        [columns, ((chips, modes, LANES), f32)],
        (decay, coef, own, other),
        scratch=[((half, tok), bf16)] * 2 + [columns],
        remote=2,
    )
    states = swap(states, ("y", "zh"))
    (got,) = call(
        both_kernel, "both", [((2, tok + chan, cols), bf16)], (own, other), remote=2
    )
    product, filtered = call(
        heads_forward_kernel,
        "heads_forward",
        [((nz, half, length), bf16), ((2, half, tok), bf16)],
        (states, decay, coef, yf, got),
        scratch=[columns],
    )

    parts = call(
        back_kernel, "back", [((all_chan // nx, tok), bf16)] * nx, (out_weight, out_grad)
    )
    product = spread(product, "zl")
    parts = [parts[0]] + [shift(part, "x", k) for k, part in enumerate(parts) if k]

    parts = call(split_kernel, "split", [gate] * nz, parts, cost=LONG)
    own, *parts, product = lax.optimization_barrier((*parts, product))
    own, other = call(
        sum_kernel,
        "sum",
        [((half, tok), f32)] * 2,
        (own, *(shift(part, "zl", k + 1) for k, part in enumerate(parts))),
    )
    product = spread(jnp.broadcast_to(product[None], (nx,) + product.shape), "x")
    yb, state, grad_outer, grad_outer_other = call(
        scan_backward_kernel,
        "scan_backward",
        [columns, ((modes, 2 * LANES), bf16)] + [((half, tok), bf16)] * 2,
        (own, other_core(other), filtered, got, decay, coef),
        scratch=[columns],
    )

    sums = (ny, nh * 2 * SUB + modes, cols)
    partial = pl.pallas_call(
        weight_kernel,
        out_shape=jax.ShapeDtypeStruct(sums, bf16),
        in_specs=[pl.BlockSpec(memory_space=pltpu.VMEM)] * 3,
        out_specs=pl.BlockSpec(memory_space=pl.ANY),
        scratch_shapes=[pltpu.VMEM(sums, bf16), pltpu.SemaphoreType.DMA((ny,))],
        compiler_params=pltpu.CompilerParams(vmem_limit_bytes=24 * 2**20),
        name="weight",
    )(product, got, state)
    partial = swap(partial, "y")
    (partial,) = call(
        middle_kernel, "middle", [((nh, 2 * SUB + modes, cols), bf16)], (partial, decay)
    )
    partial = swap(partial, "zh")
    mixed, mixed_other = call(
        mixed_kernel,
        "mixed",
        [((cols, tok), f32)] * 2,
        (product, out_weight),
        scratch=[((cols, length), f32)],
    )
    mixed, grad_outer = call(
        finish_kernel,
        "finish",
        [((tok, cols), bf16), gate],
        (mixed, other_core(mixed_other), grad_outer, other_core(grad_outer_other)),
    )
    mixed, grad_outer, partial = lax.optimization_barrier((mixed, grad_outer, partial))
    scale = 1.0 / math.sqrt(length * chips)
    late = ((half + SUB, cols), f32)
    own, other = call(
        lambda *refs: last_kernel(scale, *refs),
        "last",
        [late] * 2,
        (decay, coef, partial.reshape(nh, 2 * SUB + modes, cols), yb),
        scratch=[((nh, 2 * SUB + modes, cols), bf16), columns, columns],
        remote=2,
    )
    grad_inner, grad_value, grad_weight = call(
        end_kernel,
        "end",
        [gate, gate, ((2 * SUB, cols), f32)],
        (own, other_core(other), inner_gate, value_proj),
        scratch=[late, late, gate, gate],
        remote=4,
    )
    return (mixed, grad_outer, grad_inner, grad_value, grad_weight)


def solution(mesh):
    fine = Mesh(mesh.devices.reshape(8, 3, 2, 4, 4), ("y", "zh", "core", "x", "zl"))
    seq, col = ("y", "zh", "core"), ("x", "zl")
    return jax.shard_map(
        shards,
        mesh=fine,
        in_specs=(
            P(col, seq),
            P(col, seq),
            P(col, seq),
            P(col, None),
            P(col, None),
            P(None, col),
            P(seq, col),
        ),
        out_specs=(P(seq, col), P(col, seq), P(col, seq), P(col, seq), P(seq, col)),
        check_vma=False,
    )
```

```python
import math

import jax
import jax.numpy as jnp
from jax import lax
from jax.experimental import pallas as pl
from jax.experimental.pallas import tpu as pltpu
from jax.sharding import Mesh
from jax.sharding import PartitionSpec as P

f32 = jnp.float32
bf16 = jnp.bfloat16
SUB = 32
LANES = 128
CORE, X, ZL, Y, ZH, CHIP = "core", "x", "zl", "y", "zh", ("y", "zh")


def to_columns(tile):
    rows, width = tile.shape
    pad = jnp.zeros((LANES - rows, width), f32)
    return jnp.concatenate([tile, pad], axis=0).T


def pack_kernel(i_hbm, v_hbm, o_hbm, g_hbm, own_ref, other_ref, i_ref, v_ref, o_ref, g_ref, sems):
    fetch(sems, (i_hbm, i_ref), (v_hbm, v_ref), (o_hbm, o_ref), (g_hbm, g_ref))
    tok = g_ref.shape[0]
    half = i_ref.shape[0] // 2
    core = lax.axis_index(CORE)
    for h, ref in ((core, own_ref), (1 - core, other_ref)):
        ref[:tok] = g_ref[...]
        for b in range(half // SUB):
            src = pl.ds(pl.multiple_of(2 * SUB * b + SUB * h, SUB), SUB)
            gated = (i_ref[src, :].astype(f32) * v_ref[src, :].astype(f32)).astype(bf16)
            ref[pl.ds(tok + SUB * b, SUB), :] = gated
            ref[pl.ds(tok + half + SUB * b, SUB), :] = o_ref[src, :]


def fetch(sems, *pairs):
    copies = [pltpu.make_async_copy(src, dst, sems.at[k]) for k, (src, dst) in enumerate(pairs)]
    for copy in copies:
        copy.start()
    for copy in copies:
        copy.wait()


def both_kernel(own_hbm, other_hbm, out_ref, sems):
    core = lax.axis_index(CORE)
    fetch(sems, (own_hbm, out_ref.at[core]), (other_hbm, out_ref.at[1 - core]))


def modes_kernel(d_ref, c_ref, od_ref, oc_ref, ad_ref, ac_ref):
    chan = lax.broadcasted_iota(jnp.int32, (d_ref.shape[1], LANES), 0)
    lane = lax.broadcasted_iota(jnp.int32, (d_ref.shape[1], LANES), 1)
    for src, own, both in ((d_ref, od_ref, ad_ref), (c_ref, oc_ref, ac_ref)):
        for h in range(2):
            wanted = lane + SUB * (lane // SUB) + SUB * h
            pick = jnp.where((chan == wanted) & (lane < d_ref.shape[1] // 2), 1.0, 0.0)
            both[h] = jnp.dot(
                src[...],
                pick.astype(f32),
                precision=lax.Precision.HIGHEST,
                preferred_element_type=f32,
            )
        own[...] = both[lax.axis_index(CORE)]


def back_kernel(w_ref, g_ref, *outs):
    chan = 6 * SUB
    n = len(outs)
    rows = w_ref.shape[0] // n
    grads = g_ref[...]
    for k, ref in enumerate(outs):
        block = lax.rem(lax.axis_index(X) + k, n)
        for j in range(rows // chan):
            at = pl.ds(pl.multiple_of(block * rows + j * chan, chan), chan)
            part = lax.dot_general(
                w_ref[at, :], grads, (((1,), (1,)), ((), ())), preferred_element_type=f32
            ).astype(bf16)
            for b in range(6):
                dst = j * chan + (b % 2) * 3 * SUB + (b // 2) * SUB
                ref[pl.ds(dst, SUB), :] = part[b * SUB : (b + 1) * SUB]


def split_kernel(p0, p1, p2, p3, *outs):
    rows = p0.shape[0] // len(outs)
    for k, ref in enumerate(outs):
        block = lax.rem(lax.axis_index(ZL) + k, len(outs))
        at = pl.ds(pl.multiple_of(block * rows, rows), rows)
        total = p0[at, :].astype(f32)
        for p in (p1, p2, p3):
            total = total + p[at, :].astype(f32)
        ref[...] = total.astype(bf16)


def sum_kernel(p0, p1, p2, p3, own_ref, other_ref):
    half = own_ref.shape[0]
    core = lax.axis_index(CORE)
    for h, ref in ((core, own_ref), (1 - core, other_ref)):
        at = pl.ds(pl.multiple_of(h * half, half), half)
        total = p0[at, :].astype(f32)
        for p in (p1, p2, p3):
            total = total + p[at, :].astype(f32)
        ref[...] = total


def scan(src, y_ref, rate, coef, reverse):
    length = src.shape[0]

    def step(i, state):
        lo = length - 8 - i * 8 if reverse else i * 8
        at = pl.ds(pl.multiple_of(lo, 8), 8)
        block = src[at, :]
        rows = [None] * 8
        for t in range(8):
            u = 7 - t if reverse else t
            state = state * rate + block[u : u + 1, :]
            rows[u] = jnp.sum(state * coef, axis=0, keepdims=True)
        y_ref[at, :] = jnp.concatenate(rows, axis=0)
        return state

    return lax.fori_loop(0, length // 8, step, jnp.zeros_like(coef))


def heads(y_ref, out, state, rate, reverse):
    length = y_ref.shape[0]

    def step(i, state):
        lo = length - 8 - i * 8 if reverse else i * 8
        at = pl.ds(pl.multiple_of(lo, 8), 8)
        rows = [None] * 8
        for t in range(8):
            u = 7 - t if reverse else t
            state = state * rate
            rows[u] = jnp.sum(state, axis=0, keepdims=True)
        out[at, :] = y_ref[at, :] + jnp.concatenate(rows, axis=0)
        return state

    lax.fori_loop(0, length // 8, step, state)


def scan_forward_kernel(d_ref, c_ref, own_hbm, other_hbm, y_ref, s_ref, own_ref, other_ref, gt, sems):
    half, tok = own_ref.shape
    gated = pl.ds(tok, half)
    fetch(sems, (own_hbm.at[gated], own_ref), (other_hbm.at[gated], other_ref))
    core = lax.axis_index(CORE)
    for h, ref in ((core, own_ref), (1 - core, other_ref)):
        at = pl.ds(pl.multiple_of(h * tok, tok), tok)
        gt[at, :] = to_columns(ref[...].astype(f32))
    state = scan(gt, y_ref, jnp.exp(-d_ref[...]), c_ref[...], False)
    for m in range(s_ref.shape[0]):
        s_ref[m] = state


def heads_forward_kernel(s_ref, d_ref, c_ref, y_ref, got_ref, p_ref, f_ref, ft):
    tok = got_ref.shape[2]
    half = f_ref.shape[1]
    decay = d_ref[...]
    jump = jnp.exp(-decay * float(ft.shape[0]))
    state = jnp.zeros_like(decay)
    for m in range(s_ref.shape[0]):
        state = jnp.where(m < lax.axis_index(CHIP), state * jump + s_ref[m], state)
    heads(y_ref, ft, state * c_ref[...], jnp.exp(-decay), False)
    for h in range(2):
        at = pl.ds(h * tok, tok)
        filtered = ft[at, :].T[:half].astype(bf16)
        f_ref[h] = filtered
        product = (got_ref[h, tok + half :].astype(f32) * filtered.astype(f32)).astype(bf16)
        for q in range(p_ref.shape[0]):
            p_ref[q, :, at] = product


def scan_backward_kernel(own_ref, other_ref, f_ref, got_ref, d_ref, c_ref, yo_ref, yx_ref, s_ref, go_ref, gx_ref, bt, y_ref):
    tok = got_ref.shape[2]
    half = own_ref.shape[0]
    core = lax.axis_index(CORE)
    for h, ref, out in ((core, own_ref, go_ref), (1 - core, other_ref, gx_ref)):
        total = ref[...]
        out[...] = (total * f_ref[h].astype(f32)).astype(bf16)
        outer = got_ref[h, tok + half :].astype(f32)
        at = pl.ds(pl.multiple_of(h * tok, tok), tok)
        bt[at, :] = to_columns((total * outer).astype(bf16).astype(f32))
    state = scan(bt, y_ref, jnp.exp(-d_ref[...]), c_ref[...], True)
    put_state(s_ref, state)
    yo_ref[...] = y_ref[pl.ds(pl.multiple_of(core * tok, tok), tok), :]
    yx_ref[...] = y_ref[pl.ds(pl.multiple_of((1 - core) * tok, tok), tok), :]


def put_state(ref, state):
    first = state.astype(bf16)
    ref[:, :LANES] = first
    ref[:, LANES:] = (state - first.astype(f32)).astype(bf16)


def get_state(ref):
    both = ref.astype(f32)
    return both[:, :LANES] + both[:, LANES:]


def weight_kernel(p_ref, got_ref, s_ref, out_ref):
    tok = got_ref.shape[2]
    n = out_ref.shape[0]
    rows = p_ref.shape[0] // n
    grads = got_ref[:, :tok, :].reshape(2 * tok, -1)
    for y in range(n):
        part = jnp.dot(p_ref[pl.ds(y * rows, rows), :], grads, preferred_element_type=f32)
        out_ref[y, :rows, :] = part.astype(bf16)
        out_ref[y, rows:, :] = s_ref[...]


def middle_kernel(t_ref, d_ref, out_ref):
    n = t_ref.shape[0]
    zs, rows = out_ref.shape[0] // 2, 2 * SUB
    length = 2.0 * t_ref.shape[2]
    decay = d_ref[...]
    y, zh = lax.axis_index(Y), lax.axis_index(ZH)
    jump = jnp.exp(-decay * (zs * length))
    later = jnp.zeros_like(decay)
    here = jnp.zeros_like(decay)
    for k in range(n - 1, -1, -1):
        state = get_state(t_ref[k, zs * rows :, :])
        later = jnp.where(k > y, later * jump + state, later)
        here = jnp.where(k == y, state, here)
    for z in range(zs):
        total = t_ref[0, pl.ds(z * rows, rows), :].astype(f32)
        for k in range(1, n):
            total = total + t_ref[k, pl.ds(z * rows, rows), :].astype(f32)
        far = (zs - 1 + zh - z).astype(f32) * length
        near = jnp.maximum(zh - z - 1, 0).astype(f32) * length
        carry = jnp.exp(-decay * far) * later
        carry = jnp.where(zh > z, carry + jnp.exp(-decay * near) * here, carry)
        for h in range(2):
            out_ref[2 * z + h, :SUB, :] = total[h * SUB : (h + 1) * SUB].astype(bf16)
            put_state(out_ref.at[2 * z + h, SUB:, :], carry)


def weight_rows(w_ref, core, block, count):
    blocks = w_ref.shape[0] // (2 * SUB * count)
    rows = []
    for b in range(blocks):
        start = 2 * SUB * (block * blocks + b) + SUB * core
        rows.append(w_ref[pl.ds(pl.multiple_of(start, SUB), SUB), :])
    return jnp.concatenate(rows, axis=0)


def mixed_kernel(p_ref, w_ref, own_ref, other_ref, total):
    tok = own_ref.shape[1]
    total[...] = lax.dot_general(
        weight_rows(w_ref, lax.axis_index(CORE), 0, 1),
        p_ref[...],
        (((0,), (0,)), ((), ())),
        preferred_element_type=f32,
    )
    core = lax.axis_index(CORE)
    own_ref[...] = total[:, pl.ds(pl.multiple_of(core * tok, tok), tok)]
    other_ref[...] = total[:, pl.ds(pl.multiple_of((1 - core) * tok, tok), tok)]


def halves(core, own_ref, other_ref, count):
    for h, ref in ((core, own_ref), (1 - core, other_ref)):
        for b in range(count):
            at = pl.ds(pl.multiple_of(2 * SUB * b + SUB * h, SUB), SUB)
            yield at, ref, pl.ds(SUB * b, SUB)


def finish_kernel(m_ref, mr_ref, own_ref, other_ref, mixed_ref, go_ref):
    mixed_ref[...] = (m_ref[...] + mr_ref[...]).T.astype(bf16)
    for at, ref, src in halves(lax.axis_index(CORE), own_ref, other_ref, own_ref.shape[0] // SUB):
        go_ref[at, :] = ref[src, :]


def last_kernel(scale, d_ref, c_ref, t_hbm, yo_hbm, yx_hbm, i_hbm, v_hbm, gi_ref, gv_ref, gw_ref, t_ref, yo_ref, yx_ref, i_ref, v_ref, bt, sems):
    fetch(sems, (t_hbm, t_ref), (yo_hbm, yo_ref), (yx_hbm, yx_ref), (i_hbm, i_ref), (v_hbm, v_ref))
    tok = yo_ref.shape[0]
    half = i_ref.shape[0] // 2
    core = lax.axis_index(CORE)
    later = (1 - core).astype(f32) * tok
    for h, y_ref in ((core, yo_ref), (1 - core, yx_ref)):
        state = get_state(t_ref[h, SUB:, :])
        total = t_ref[h, :SUB, :].astype(f32)
        for z in range(1, t_ref.shape[0] // 2):
            state = state + get_state(t_ref[2 * z + h, SUB:, :])
            total = total + t_ref[2 * z + h, :SUB, :].astype(f32)
        gw_ref[pl.ds(pl.multiple_of(SUB * h, SUB), SUB), :] = total * scale
        decay = d_ref[h]
        state = state * jnp.exp(-decay * later) * c_ref[h]
        heads(y_ref, bt, state, jnp.exp(-decay), True)
        back = bt[...].T[:half].astype(bf16).astype(f32)
        for b in range(half // SUB):
            at = pl.ds(pl.multiple_of(2 * SUB * b + SUB * h, SUB), SUB)
            part = back[SUB * b : SUB * (b + 1)]
            gi_ref[at, :] = (part * v_ref[at, :].astype(f32)).astype(bf16)
            gv_ref[at, :] = (part * i_ref[at, :].astype(f32)).astype(bf16)


def call(kernel, name, outs, args, scratch=(), cost=None, remote=0, limit=24):
    specs = [pl.BlockSpec(memory_space=pltpu.VMEM)] * (len(args) - remote)
    specs += [pl.BlockSpec(memory_space=pl.ANY)] * remote
    return pl.pallas_call(
        kernel,
        out_shape=tuple(jax.ShapeDtypeStruct(s, t) for s, t in outs),
        in_specs=specs,
        out_specs=tuple([pl.BlockSpec(memory_space=pltpu.VMEM)] * len(outs)),
        scratch_shapes=[pltpu.VMEM(s, t) for s, t in scratch]
        + ([pltpu.SemaphoreType.DMA((remote,))] if remote else []),
        compiler_params=None if limit is None else pltpu.CompilerParams(vmem_limit_bytes=limit * 2**20),
        cost_estimate=cost,
        name=name,
    )(*args)


LONG = pl.CostEstimate(flops=10**11, bytes_accessed=0, transcendentals=0)


def swap(x, axes):
    return lax.all_to_all(x, axes, 0, 0, tiled=True)


def spread(x, axis):
    n, rows, m = x.shape
    return swap(x.reshape(n * rows, m), axis)


def shift(x, axis, k):
    n = lax.axis_size(axis)
    return lax.ppermute(x, axis, [(i, (i + k) % n) for i in range(n)])


def other_core(x):
    return lax.ppermute(x, "core", [(0, 1), (1, 0)])


def shards(outer_gate, inner_gate, value_proj, residues, decays, out_weight, out_grad):
    chan, tok = outer_gate.shape
    half = chan // 2
    length = 2 * tok
    all_chan, cols = out_weight.shape
    modes = decays.shape[1]
    ny, nh, nx, nz = (lax.axis_size(axis) for axis in ("y", "zh", "x", "zl"))
    chips = ny * nh

    packed = ((tok + chan, cols), bf16)
    gate = ((chan, tok), bf16)
    own, other = call(
        pack_kernel,
        "pack",
        [packed] * 2,
        (inner_gate, value_proj, outer_gate, out_grad),
        scratch=[gate] * 3 + [((tok, cols), bf16)],
        remote=4,
        limit=None,
    )
    other = other_core(other)
    coef = residues * jnp.sqrt(-jnp.expm1(-2.0 * decays))
    small = ((modes, LANES), f32)
    pair = ((2, modes, LANES), f32)
    decay, coef, decay_both, coef_both = call(
        modes_kernel, "modes", [small, small, pair, pair], (decays.T, coef.T)
    )

    columns = ((length, LANES), f32)
    yf, states = call(
        scan_forward_kernel,
        "scan_forward",
        [columns, ((chips, modes, LANES), f32)],
        (decay, coef, own, other),
        scratch=[((half, tok), bf16)] * 2 + [columns],
        remote=2,
    )
    states = swap(states, ("y", "zh"))
    (got,) = call(
        both_kernel, "both", [((2, tok + chan, cols), bf16)], (own, other), remote=2
    )
    product, filtered = call(
        heads_forward_kernel,
        "heads_forward",
        [((nz, half, length), bf16), ((2, half, tok), bf16)],
        (states, decay, coef, yf, got),
        scratch=[columns],
    )

    parts = call(
        back_kernel, "back", [((all_chan // nx, tok), bf16)] * nx, (out_weight, out_grad)
    )
    product = spread(product, "zl")
    parts = [parts[0]] + [shift(part, "x", k) for k, part in enumerate(parts) if k]

    parts = call(split_kernel, "split", [gate] * nz, parts, cost=LONG)
    own, *parts, product = lax.optimization_barrier((*parts, product))
    own, other = call(
        sum_kernel,
        "sum",
        [((half, tok), f32)] * 2,
        (own, *(shift(part, "zl", k + 1) for k, part in enumerate(parts))),
    )
    product = spread(jnp.broadcast_to(product[None], (nx,) + product.shape), "x")
    half_columns = ((tok, LANES), f32)
    yb, yb_other, state, grad_outer, grad_outer_other = call(
        scan_backward_kernel,
        "scan_backward",
        [half_columns] * 2 + [((modes, 2 * LANES), bf16)] + [((half, tok), bf16)] * 2,
        (own, other_core(other), filtered, got, decay, coef),
        scratch=[columns] * 2,
    )

    (partial,) = call(
        weight_kernel,
        "weight",
        [((ny, nh * 2 * SUB + modes, cols), bf16)],
        (product, got, state),
    )
    partial = swap(partial, "y")
    last = ((2 * nh, SUB + modes, cols), bf16)
    (partial,) = call(middle_kernel, "middle", [last], (partial, decay))
    partial = swap(partial, ("zh", "core"))
    mixed, mixed_other = call(
        mixed_kernel,
        "mixed",
        [((cols, tok), f32)] * 2,
        (product, out_weight),
        scratch=[((cols, length), f32)],
    )
    mixed, grad_outer = call(
        finish_kernel,
        "finish",
        [((tok, cols), bf16), gate],
        (mixed, other_core(mixed_other), grad_outer, other_core(grad_outer_other)),
    )
    mixed, grad_outer, partial = lax.optimization_barrier((mixed, grad_outer, partial))
    scale = 1.0 / math.sqrt(length * chips)
    grad_inner, grad_value, grad_weight = call(
        lambda *refs: last_kernel(scale, *refs),
        "last",
        [gate, gate, ((2 * SUB, cols), f32)],
        (
            decay_both,
            coef_both,
            partial.reshape(last[0]),
            yb,
            other_core(yb_other),
            inner_gate,
            value_proj,
        ),
        scratch=[last, half_columns, half_columns, gate, gate, half_columns],
        remote=5,
    )
    return (mixed, grad_outer, grad_inner, grad_value, grad_weight)


def solution(mesh):
    fine = Mesh(mesh.devices.reshape(8, 3, 2, 4, 4), ("y", "zh", "core", "x", "zl"))
    seq, col = ("y", "zh", "core"), ("x", "zl")
    return jax.shard_map(
        shards,
        mesh=fine,
        in_specs=(
            P(col, seq),
            P(col, seq),
            P(col, seq),
            P(col, None),
            P(col, None),
            P(None, col),
            P(seq, col),
        ),
        out_specs=(P(seq, col), P(col, seq), P(col, seq), P(col, seq), P(seq, col)),
        check_vma=False,
    )
```

```python
import math

import jax
import jax.numpy as jnp
from jax import lax
from jax.experimental import pallas as pl
from jax.experimental.pallas import tpu as pltpu
from jax.sharding import Mesh
from jax.sharding import PartitionSpec as P

f32 = jnp.float32
bf16 = jnp.bfloat16
SUB = 32
LANES = 128
CORE, X, ZL, Y, ZH, CHIP = "core", "x", "zl", "y", "zh", ("y", "zh")


def to_columns(tile):
    rows, width = tile.shape
    pad = jnp.zeros((LANES - rows, width), f32)
    return jnp.concatenate([tile, pad], axis=0).T


def pack_kernel(i_hbm, v_hbm, o_hbm, g_hbm, own_ref, other_ref, i_ref, v_ref, o_ref, g_ref, sems):
    fetch(sems, (i_hbm, i_ref), (v_hbm, v_ref), (o_hbm, o_ref), (g_hbm, g_ref))
    tok = g_ref.shape[0]
    half = i_ref.shape[0] // 2
    core = lax.axis_index(CORE)
    for h, ref in ((core, own_ref), (1 - core, other_ref)):
        ref[:tok] = g_ref[...]
        for b in range(half // SUB):
            src = pl.ds(pl.multiple_of(2 * SUB * b + SUB * h, SUB), SUB)
            gated = (i_ref[src, :].astype(f32) * v_ref[src, :].astype(f32)).astype(bf16)
            ref[pl.ds(tok + SUB * b, SUB), :] = gated
            ref[pl.ds(tok + half + SUB * b, SUB), :] = o_ref[src, :]


def fetch(sems, *pairs):
    copies = [pltpu.make_async_copy(src, dst, sems.at[k]) for k, (src, dst) in enumerate(pairs)]
    for copy in copies:
        copy.start()
    for copy in copies:
        copy.wait()


def both_kernel(own_hbm, other_hbm, out_ref, sems):
    core = lax.axis_index(CORE)
    fetch(sems, (own_hbm, out_ref.at[core]), (other_hbm, out_ref.at[1 - core]))


def modes_kernel(d_ref, c_ref, od_ref, oc_ref, ad_ref, ac_ref):
    chan = lax.broadcasted_iota(jnp.int32, (d_ref.shape[1], LANES), 0)
    lane = lax.broadcasted_iota(jnp.int32, (d_ref.shape[1], LANES), 1)
    for src, own, both in ((d_ref, od_ref, ad_ref), (c_ref, oc_ref, ac_ref)):
        for h in range(2):
            wanted = lane + SUB * (lane // SUB) + SUB * h
            pick = jnp.where((chan == wanted) & (lane < d_ref.shape[1] // 2), 1.0, 0.0)
            both[h] = jnp.dot(
                src[...],
                pick.astype(f32),
                precision=lax.Precision.HIGHEST,
                preferred_element_type=f32,
            )
        own[...] = both[lax.axis_index(CORE)]


def back_kernel(w_ref, g_ref, *outs):
    chan = 6 * SUB
    n = len(outs)
    rows = w_ref.shape[0] // n
    grads = g_ref[...]
    for k, ref in enumerate(outs):
        block = lax.rem(lax.axis_index(X) + k, n)
        for j in range(rows // chan):
            at = pl.ds(pl.multiple_of(block * rows + j * chan, chan), chan)
            part = lax.dot_general(
                w_ref[at, :], grads, (((1,), (1,)), ((), ())), preferred_element_type=f32
            ).astype(bf16)
            for b in range(6):
                dst = j * chan + (b % 2) * 3 * SUB + (b // 2) * SUB
                ref[pl.ds(dst, SUB), :] = part[b * SUB : (b + 1) * SUB]


def split_kernel(p0, p1, p2, p3, *outs):
    rows = p0.shape[0] // len(outs)
    for k, ref in enumerate(outs):
        block = lax.rem(lax.axis_index(ZL) + k, len(outs))
        at = pl.ds(pl.multiple_of(block * rows, rows), rows)
        total = p0[at, :].astype(f32)
        for p in (p1, p2, p3):
            total = total + p[at, :].astype(f32)
        ref[...] = total.astype(bf16)


def sum_kernel(p0, p1, p2, p3, own_ref, other_ref):
    half = own_ref.shape[0]
    core = lax.axis_index(CORE)
    for h, ref in ((core, own_ref), (1 - core, other_ref)):
        at = pl.ds(pl.multiple_of(h * half, half), half)
        total = p0[at, :].astype(f32)
        for p in (p1, p2, p3):
            total = total + p[at, :].astype(f32)
        ref[...] = total


def scan(src, y_ref, rate, coef, reverse):
    length = src.shape[0]

    def step(i, state):
        lo = length - 8 - i * 8 if reverse else i * 8
        at = pl.ds(pl.multiple_of(lo, 8), 8)
        block = src[at, :]
        rows = [None] * 8
        for t in range(8):
            u = 7 - t if reverse else t
            state = state * rate + block[u : u + 1, :]
            rows[u] = jnp.sum(state * coef, axis=0, keepdims=True)
        y_ref[at, :] = jnp.concatenate(rows, axis=0)
        return state

    return lax.fori_loop(0, length // 8, step, jnp.zeros_like(coef))


def heads(y_ref, out, state, rate, reverse):
    length = y_ref.shape[0]

    def step(i, state):
        lo = length - 8 - i * 8 if reverse else i * 8
        at = pl.ds(pl.multiple_of(lo, 8), 8)
        rows = [None] * 8
        for t in range(8):
            u = 7 - t if reverse else t
            state = state * rate
            rows[u] = jnp.sum(state, axis=0, keepdims=True)
        out[at, :] = y_ref[at, :] + jnp.concatenate(rows, axis=0)
        return state

    lax.fori_loop(0, length // 8, step, state)


def scan_forward_kernel(d_ref, c_ref, own_hbm, other_hbm, y_ref, s_ref, own_ref, other_ref, gt, sems):
    half, tok = own_ref.shape
    gated = pl.ds(tok, half)
    fetch(sems, (own_hbm.at[gated], own_ref), (other_hbm.at[gated], other_ref))
    core = lax.axis_index(CORE)
    for h, ref in ((core, own_ref), (1 - core, other_ref)):
        at = pl.ds(pl.multiple_of(h * tok, tok), tok)
        gt[at, :] = to_columns(ref[...].astype(f32))
    state = scan(gt, y_ref, jnp.exp(-d_ref[...]), c_ref[...], False)
    for m in range(s_ref.shape[0]):
        s_ref[m] = state


def heads_forward_kernel(s_ref, d_ref, c_ref, y_ref, got_ref, p_ref, f_ref, ft):
    tok = got_ref.shape[2]
    half = f_ref.shape[1]
    decay = d_ref[...]
    jump = jnp.exp(-decay * float(ft.shape[0]))
    state = jnp.zeros_like(decay)
    for m in range(s_ref.shape[0]):
        state = jnp.where(m < lax.axis_index(CHIP), state * jump + s_ref[m], state)
    heads(y_ref, ft, state * c_ref[...], jnp.exp(-decay), False)
    for h in range(2):
        at = pl.ds(h * tok, tok)
        filtered = ft[at, :].T[:half].astype(bf16)
        f_ref[h] = filtered
        product = (got_ref[h, tok + half :].astype(f32) * filtered.astype(f32)).astype(bf16)
        for q in range(p_ref.shape[0]):
            p_ref[q, :, at] = product


def scan_backward_kernel(own_ref, other_ref, f_ref, got_ref, d_ref, c_ref, yo_ref, yx_ref, s_ref, go_ref, gx_ref, bt, y_ref):
    tok = got_ref.shape[2]
    half = own_ref.shape[0]
    core = lax.axis_index(CORE)
    for h, ref, out in ((core, own_ref, go_ref), (1 - core, other_ref, gx_ref)):
        total = ref[...]
        out[...] = (total * f_ref[h].astype(f32)).astype(bf16)
        outer = got_ref[h, tok + half :].astype(f32)
        at = pl.ds(pl.multiple_of(h * tok, tok), tok)
        bt[at, :] = to_columns((total * outer).astype(bf16).astype(f32))
    state = scan(bt, y_ref, jnp.exp(-d_ref[...]), c_ref[...], True)
    put_state(s_ref, state)
    yo_ref[...] = y_ref[pl.ds(pl.multiple_of(core * tok, tok), tok), :]
    yx_ref[...] = y_ref[pl.ds(pl.multiple_of((1 - core) * tok, tok), tok), :]


def put_state(ref, state):
    first = state.astype(bf16)
    ref[:, :LANES] = first
    ref[:, LANES:] = (state - first.astype(f32)).astype(bf16)


def get_state(ref):
    both = ref.astype(f32)
    return both[:, :LANES] + both[:, LANES:]


def weight_kernel(p_ref, got_ref, s_ref, out_ref):
    tok = got_ref.shape[2]
    n = out_ref.shape[0]
    rows = p_ref.shape[0] // n
    grads = got_ref[:, :tok, :].reshape(2 * tok, -1)
    for y in range(n):
        part = jnp.dot(p_ref[pl.ds(y * rows, rows), :], grads, preferred_element_type=f32)
        out_ref[y, :rows, :] = part.astype(bf16)
        out_ref[y, rows:, :] = s_ref[...]


def middle_kernel(t_ref, d_ref, out_ref):
    n = t_ref.shape[0]
    zs, rows = out_ref.shape[0] // 2, 2 * SUB
    length = 2.0 * t_ref.shape[2]
    decay = d_ref[...]
    y, zh = lax.axis_index(Y), lax.axis_index(ZH)
    jump = jnp.exp(-decay * (zs * length))
    later = jnp.zeros_like(decay)
    here = jnp.zeros_like(decay)
    for k in range(n - 1, -1, -1):
        state = get_state(t_ref[k, zs * rows :, :])
        later = jnp.where(k > y, later * jump + state, later)
        here = jnp.where(k == y, state, here)
    for z in range(zs):
        total = t_ref[0, pl.ds(z * rows, rows), :].astype(f32)
        for k in range(1, n):
            total = total + t_ref[k, pl.ds(z * rows, rows), :].astype(f32)
        far = (zs - 1 + zh - z).astype(f32) * length
        near = jnp.maximum(zh - z - 1, 0).astype(f32) * length
        carry = jnp.exp(-decay * far) * later
        carry = jnp.where(zh > z, carry + jnp.exp(-decay * near) * here, carry)
        for h in range(2):
            out_ref[2 * z + h, :SUB, :] = total[h * SUB : (h + 1) * SUB].astype(bf16)
            put_state(out_ref.at[2 * z + h, SUB:, :], carry)


def weight_rows(w_ref, core, block, count):
    blocks = w_ref.shape[0] // (2 * SUB * count)
    rows = []
    for b in range(blocks):
        start = 2 * SUB * (block * blocks + b) + SUB * core
        rows.append(w_ref[pl.ds(pl.multiple_of(start, SUB), SUB), :])
    return jnp.concatenate(rows, axis=0)


def mixed_kernel(p_ref, w_ref, y_ref, g_ref, own_ref, other_ref, total):
    cols, tok = own_ref.shape
    total[...] = lax.dot_general(
        weight_rows(w_ref, lax.axis_index(CORE), 0, 1),
        p_ref[...],
        (((0,), (0,)), ((), ())),
        preferred_element_type=f32,
    )
    core = lax.axis_index(CORE)
    own_ref[...] = total[:, pl.ds(pl.multiple_of(core * tok, tok), tok)]
    other_ref[:cols, :tok] = total[:, pl.ds(pl.multiple_of((1 - core) * tok, tok), tok)]
    other_ref[:cols, tok:] = y_ref[...]
    other_ref[cols:, :tok] = g_ref[...].astype(f32)


def halves(core, own_ref, other_ref, count):
    for h, ref in ((core, own_ref), (1 - core, other_ref)):
        for b in range(count):
            at = pl.ds(pl.multiple_of(2 * SUB * b + SUB * h, SUB), SUB)
            yield at, ref, pl.ds(SUB * b, SUB)


def finish_kernel(m_ref, x_ref, g_ref, mixed_ref, go_ref):
    cols, tok = m_ref.shape
    mixed_ref[...] = (m_ref[...] + x_ref[:cols, :tok]).T.astype(bf16)
    core = lax.axis_index(CORE)
    for at, ref, src in halves(core, g_ref, x_ref.at[cols:, :tok], g_ref.shape[0] // SUB):
        go_ref[at, :] = ref[src, :].astype(bf16)


def last_kernel(scale, t_hbm, yo_hbm, x_hbm, i_hbm, v_hbm, d_hbm, c_hbm, gi_ref, gv_ref, gw_ref, t_ref, yo_ref, yx_ref, i_ref, v_ref, d_ref, c_ref, bt, sems):
    tok, lanes = yx_ref.shape
    part = x_hbm.at[pl.ds(0, tok), pl.ds(tok, lanes)]
    pairs = ((t_hbm, t_ref), (yo_hbm, yo_ref), (part, yx_ref), (i_hbm, i_ref), (v_hbm, v_ref))
    fetch(sems, *pairs, (d_hbm, d_ref), (c_hbm, c_ref))
    half = i_ref.shape[0] // 2
    core = lax.axis_index(CORE)
    later = (1 - core).astype(f32) * tok
    for h, y_ref in ((core, yo_ref), (1 - core, yx_ref)):
        state = get_state(t_ref[h, SUB:, :])
        total = t_ref[h, :SUB, :].astype(f32)
        for z in range(1, t_ref.shape[0] // 2):
            state = state + get_state(t_ref[2 * z + h, SUB:, :])
            total = total + t_ref[2 * z + h, :SUB, :].astype(f32)
        gw_ref[pl.ds(pl.multiple_of(SUB * h, SUB), SUB), :] = total * scale
        decay = d_ref[h]
        state = state * jnp.exp(-decay * later) * c_ref[h]
        heads(y_ref, bt, state, jnp.exp(-decay), True)
        back = bt[...].T[:half].astype(bf16).astype(f32)
        for b in range(half // SUB):
            at = pl.ds(pl.multiple_of(2 * SUB * b + SUB * h, SUB), SUB)
            part = back[SUB * b : SUB * (b + 1)]
            gi_ref[at, :] = (part * v_ref[at, :].astype(f32)).astype(bf16)
            gv_ref[at, :] = (part * i_ref[at, :].astype(f32)).astype(bf16)


def call(kernel, name, outs, args, scratch=(), cost=None, remote=0, limit=24):
    specs = [pl.BlockSpec(memory_space=pltpu.VMEM)] * (len(args) - remote)
    specs += [pl.BlockSpec(memory_space=pl.ANY)] * remote
    return pl.pallas_call(
        kernel,
        out_shape=tuple(jax.ShapeDtypeStruct(s, t) for s, t in outs),
        in_specs=specs,
        out_specs=tuple([pl.BlockSpec(memory_space=pltpu.VMEM)] * len(outs)),
        scratch_shapes=[pltpu.VMEM(s, t) for s, t in scratch]
        + ([pltpu.SemaphoreType.DMA((remote,))] if remote else []),
        compiler_params=None if limit is None else pltpu.CompilerParams(vmem_limit_bytes=limit * 2**20),
        cost_estimate=cost,
        name=name,
    )(*args)


LONG = pl.CostEstimate(flops=10**11, bytes_accessed=0, transcendentals=0)


def swap(x, axes):
    return lax.all_to_all(x, axes, 0, 0, tiled=True)


def spread(x, axis):
    n, rows, m = x.shape
    return swap(x.reshape(n * rows, m), axis)


def shift(x, axis, k):
    n = lax.axis_size(axis)
    return lax.ppermute(x, axis, [(i, (i + k) % n) for i in range(n)])


def other_core(x):
    return lax.ppermute(x, "core", [(0, 1), (1, 0)])


def shards(outer_gate, inner_gate, value_proj, residues, decays, out_weight, out_grad):
    chan, tok = outer_gate.shape
    half = chan // 2
    length = 2 * tok
    all_chan, cols = out_weight.shape
    modes = decays.shape[1]
    ny, nh, nx, nz = (lax.axis_size(axis) for axis in ("y", "zh", "x", "zl"))
    chips = ny * nh

    packed = ((tok + chan, cols), bf16)
    gate = ((chan, tok), bf16)
    own, other = call(
        pack_kernel,
        "pack",
        [packed] * 2,
        (inner_gate, value_proj, outer_gate, out_grad),
        scratch=[gate] * 3 + [((tok, cols), bf16)],
        remote=4,
        limit=None,
    )
    other = other_core(other)
    coef = residues * jnp.sqrt(-jnp.expm1(-2.0 * decays))
    small = ((modes, LANES), f32)
    pair = ((2, modes, LANES), f32)
    decay, coef, decay_both, coef_both = call(
        modes_kernel, "modes", [small, small, pair, pair], (decays.T, coef.T)
    )

    columns = ((length, LANES), f32)
    yf, states = call(
        scan_forward_kernel,
        "scan_forward",
        [columns, ((chips, modes, LANES), f32)],
        (decay, coef, own, other),
        scratch=[((half, tok), bf16)] * 2 + [columns],
        remote=2,
    )
    states = swap(states, ("y", "zh"))
    (got,) = call(
        both_kernel, "both", [((2, tok + chan, cols), bf16)], (own, other), remote=2
    )
    product, filtered = call(
        heads_forward_kernel,
        "heads_forward",
        [((nz, half, length), bf16), ((2, half, tok), bf16)],
        (states, decay, coef, yf, got),
        scratch=[columns],
    )

    parts = call(
        back_kernel, "back", [((all_chan // nx, tok), bf16)] * nx, (out_weight, out_grad)
    )
    product = spread(product, "zl")
    parts = [parts[0]] + [shift(part, "x", k) for k, part in enumerate(parts) if k]

    parts = call(split_kernel, "split", [gate] * nz, parts, cost=LONG)
    own, *parts, product = lax.optimization_barrier((*parts, product))
    own, other = call(
        sum_kernel,
        "sum",
        [((half, tok), f32)] * 2,
        (own, *(shift(part, "zl", k + 1) for k, part in enumerate(parts))),
    )
    product = spread(jnp.broadcast_to(product[None], (nx,) + product.shape), "x")
    half_columns = ((tok, LANES), f32)
    yb, yb_other, state, grad_outer, grad_outer_other = call(
        scan_backward_kernel,
        "scan_backward",
        [half_columns] * 2 + [((modes, 2 * LANES), bf16)] + [((half, tok), bf16)] * 2,
        (own, other_core(other), filtered, got, decay, coef),
        scratch=[columns] * 2,
    )

    (partial,) = call(
        weight_kernel,
        "weight",
        [((ny, nh * 2 * SUB + modes, cols), bf16)],
        (product, got, state),
    )
    partial = swap(partial, "y")
    last = ((2 * nh, SUB + modes, cols), bf16)
    (partial,) = call(middle_kernel, "middle", [last], (partial, decay))
    partial = swap(partial, ("zh", "core"))
    mixed, mixed_other = call(
        mixed_kernel,
        "mixed",
        [((cols, tok), f32), ((cols + half, tok + LANES), f32)],
        (product, out_weight, yb_other, grad_outer_other),
        scratch=[((cols, length), f32)],
    )
    got = other_core(mixed_other)
    mixed, grad_outer = call(
        finish_kernel,
        "finish",
        [((tok, cols), bf16), gate],
        (mixed, got, grad_outer),
    )
    mixed, grad_outer, partial = lax.optimization_barrier((mixed, grad_outer, partial))
    scale = 1.0 / math.sqrt(length * chips)
    grad_inner, grad_value, grad_weight = call(
        lambda *refs: last_kernel(scale, *refs),
        "last",
        [gate, gate, ((2 * SUB, cols), f32)],
        (partial.reshape(last[0]), yb, got, inner_gate, value_proj, decay_both, coef_both),
        scratch=[last, half_columns, half_columns, gate, gate, pair, pair, half_columns],
        remote=7,
    )
    return (mixed, grad_outer, grad_inner, grad_value, grad_weight)


def solution(mesh):
    fine = Mesh(mesh.devices.reshape(8, 3, 2, 4, 4), ("y", "zh", "core", "x", "zl"))
    seq, col = ("y", "zh", "core"), ("x", "zl")
    return jax.shard_map(
        shards,
        mesh=fine,
        in_specs=(
            P(col, seq),
            P(col, seq),
            P(col, seq),
            P(col, None),
            P(col, None),
            P(None, col),
            P(seq, col),
        ),
        out_specs=(P(seq, col), P(col, seq), P(col, seq), P(col, seq), P(seq, col)),
        check_vma=False,
    )
```

```python
import math

import jax
import jax.numpy as jnp
from jax import lax
from jax.experimental import pallas as pl
from jax.experimental.pallas import tpu as pltpu
from jax.sharding import Mesh
from jax.sharding import PartitionSpec as P

f32 = jnp.float32
bf16 = jnp.bfloat16
SUB = 32
LANES = 128
CORE, X, ZL, Y, ZH, CHIP = "core", "x", "zl", "y", "zh", ("y", "zh")


def to_columns(tile):
    rows, width = tile.shape
    pad = jnp.zeros((LANES - rows, width), f32)
    return jnp.concatenate([tile, pad], axis=0).T


def pack_kernel(i_hbm, v_hbm, o_hbm, g_hbm, own_ref, other_ref, i_ref, v_ref, o_ref, g_ref, sems):
    fetch(sems, (i_hbm, i_ref), (v_hbm, v_ref), (o_hbm, o_ref), (g_hbm, g_ref))
    tok = g_ref.shape[0]
    half = i_ref.shape[0] // 2
    core = lax.axis_index(CORE)
    for h, ref in ((core, own_ref), (1 - core, other_ref)):
        ref[:tok] = g_ref[...]
        for b in range(half // SUB):
            src = pl.ds(pl.multiple_of(2 * SUB * b + SUB * h, SUB), SUB)
            gated = (i_ref[src, :].astype(f32) * v_ref[src, :].astype(f32)).astype(bf16)
            ref[pl.ds(tok + SUB * b, SUB), :] = gated
            ref[pl.ds(tok + half + SUB * b, SUB), :] = o_ref[src, :]


def fetch(sems, *pairs):
    copies = [pltpu.make_async_copy(src, dst, sems.at[k]) for k, (src, dst) in enumerate(pairs)]
    for copy in copies:
        copy.start()
    for copy in copies:
        copy.wait()


def both_kernel(own_hbm, other_hbm, out_ref, sems):
    core = lax.axis_index(CORE)
    fetch(sems, (own_hbm, out_ref.at[core]), (other_hbm, out_ref.at[1 - core]))


def modes_kernel(d_ref, c_ref, od_ref, oc_ref, ad_ref, ac_ref):
    chan = lax.broadcasted_iota(jnp.int32, (d_ref.shape[1], LANES), 0)
    lane = lax.broadcasted_iota(jnp.int32, (d_ref.shape[1], LANES), 1)
    for src, own, both in ((d_ref, od_ref, ad_ref), (c_ref, oc_ref, ac_ref)):
        for h in range(2):
            wanted = lane + SUB * (lane // SUB) + SUB * h
            pick = jnp.where((chan == wanted) & (lane < d_ref.shape[1] // 2), 1.0, 0.0)
            both[h] = jnp.dot(
                src[...],
                pick.astype(f32),
                precision=lax.Precision.HIGHEST,
                preferred_element_type=f32,
            )
        own[...] = both[lax.axis_index(CORE)]


def back_kernel(w_ref, g_ref, *outs):
    chan = 6 * SUB
    n = len(outs)
    rows = w_ref.shape[0] // n
    grads = g_ref[...]
    for k, ref in enumerate(outs):
        block = lax.rem(lax.axis_index(X) + k, n)
        for j in range(rows // chan):
            at = pl.ds(pl.multiple_of(block * rows + j * chan, chan), chan)
            part = lax.dot_general(
                w_ref[at, :], grads, (((1,), (1,)), ((), ())), preferred_element_type=f32
            ).astype(bf16)
            for b in range(6):
                dst = j * chan + (b % 2) * 3 * SUB + (b // 2) * SUB
                ref[pl.ds(dst, SUB), :] = part[b * SUB : (b + 1) * SUB]


def split_kernel(p0, p1, p2, p3, *outs):
    rows = p0.shape[0] // len(outs)
    for k, ref in enumerate(outs):
        block = lax.rem(lax.axis_index(ZL) + k, len(outs))
        at = pl.ds(pl.multiple_of(block * rows, rows), rows)
        total = p0[at, :].astype(f32)
        for p in (p1, p2, p3):
            total = total + p[at, :].astype(f32)
        ref[...] = total.astype(bf16)


def sum_kernel(p0, p1, p2, p3, own_ref, other_ref):
    half = own_ref.shape[0]
    core = lax.axis_index(CORE)
    for h, ref in ((core, own_ref), (1 - core, other_ref)):
        at = pl.ds(pl.multiple_of(h * half, half), half)
        total = p0[at, :].astype(f32)
        for p in (p1, p2, p3):
            total = total + p[at, :].astype(f32)
        ref[...] = total


def scan(src, y_ref, rate, coef, reverse):
    length = src.shape[0]

    def step(i, state):
        lo = length - 8 - i * 8 if reverse else i * 8
        at = pl.ds(pl.multiple_of(lo, 8), 8)
        block = src[at, :]
        rows = [None] * 8
        for t in range(8):
            u = 7 - t if reverse else t
            state = state * rate + block[u : u + 1, :]
            rows[u] = jnp.sum(state * coef, axis=0, keepdims=True)
        y_ref[at, :] = jnp.concatenate(rows, axis=0)
        return state

    return lax.fori_loop(0, length // 8, step, jnp.zeros_like(coef))


def heads(y_ref, out, state, rate, reverse):
    length = y_ref.shape[0]

    def step(i, state):
        lo = length - 8 - i * 8 if reverse else i * 8
        at = pl.ds(pl.multiple_of(lo, 8), 8)
        rows = [None] * 8
        for t in range(8):
            u = 7 - t if reverse else t
            state = state * rate
            rows[u] = jnp.sum(state, axis=0, keepdims=True)
        out[at, :] = y_ref[at, :] + jnp.concatenate(rows, axis=0)
        return state

    lax.fori_loop(0, length // 8, step, state)


def scan_forward_kernel(d_ref, c_ref, own_hbm, other_hbm, y_ref, s_ref, own_ref, other_ref, gt, sems):
    half, tok = own_ref.shape
    gated = pl.ds(tok, half)
    fetch(sems, (own_hbm.at[gated], own_ref), (other_hbm.at[gated], other_ref))
    core = lax.axis_index(CORE)
    for h, ref in ((core, own_ref), (1 - core, other_ref)):
        at = pl.ds(pl.multiple_of(h * tok, tok), tok)
        gt[at, :] = to_columns(ref[...].astype(f32))
    state = scan(gt, y_ref, jnp.exp(-d_ref[...]), c_ref[...], False)
    for m in range(s_ref.shape[0]):
        s_ref[m] = state


def heads_forward_kernel(s_ref, d_ref, c_ref, y_ref, got_ref, p_ref, f_ref, ft):
    tok = got_ref.shape[2]
    half = f_ref.shape[1]
    decay = d_ref[...]
    jump = jnp.exp(-decay * float(ft.shape[0]))
    state = jnp.zeros_like(decay)
    chips = s_ref.shape[0]
    for m in range(chips):
        state = jnp.where(m < lax.axis_index(CHIP), state * jump + s_ref[chips - 1 - m], state)
    heads(y_ref, ft, state * c_ref[...], jnp.exp(-decay), False)
    for h in range(2):
        at = pl.ds(h * tok, tok)
        filtered = ft[at, :].T[:half].astype(bf16)
        f_ref[h] = filtered
        product = (got_ref[h, tok + half :].astype(f32) * filtered.astype(f32)).astype(bf16)
        for q in range(p_ref.shape[0]):
            p_ref[q, :, at] = product


def scan_backward_kernel(own_ref, other_ref, f_ref, got_ref, d_ref, c_ref, yo_ref, yx_ref, s_ref, go_ref, gx_ref, bt, y_ref):
    tok = got_ref.shape[2]
    half = own_ref.shape[0]
    core = lax.axis_index(CORE)
    for h, ref, out in ((core, own_ref, go_ref), (1 - core, other_ref, gx_ref)):
        total = ref[...]
        out[...] = (total * f_ref[h].astype(f32)).astype(bf16)
        outer = got_ref[h, tok + half :].astype(f32)
        at = pl.ds(pl.multiple_of(h * tok, tok), tok)
        bt[at, :] = to_columns((total * outer).astype(bf16).astype(f32))
    state = scan(bt, y_ref, jnp.exp(-d_ref[...]), c_ref[...], True)
    put_state(s_ref, state)
    yo_ref[...] = y_ref[pl.ds(pl.multiple_of(core * tok, tok), tok), :]
    yx_ref[...] = y_ref[pl.ds(pl.multiple_of((1 - core) * tok, tok), tok), :]


def put_state(ref, state):
    first = state.astype(bf16)
    ref[:, :LANES] = first
    ref[:, LANES:] = (state - first.astype(f32)).astype(bf16)


def get_state(ref):
    both = ref.astype(f32)
    return both[:, :LANES] + both[:, LANES:]


def weight_kernel(p_ref, got_ref, s_ref, out_ref):
    tok = got_ref.shape[2]
    n = out_ref.shape[0]
    rows = p_ref.shape[0] // n
    grads = got_ref[:, :tok, :].reshape(2 * tok, -1)
    for y in range(n):
        part = jnp.dot(p_ref[pl.ds(y * rows, rows), :], grads, preferred_element_type=f32)
        out_ref[n - 1 - y, :rows, :] = part.astype(bf16)
        out_ref[n - 1 - y, rows:, :] = s_ref[...]


def middle_kernel(t_ref, d_ref, out_ref):
    n = t_ref.shape[0]
    zs, rows = out_ref.shape[0] // 2, 2 * SUB
    length = 2.0 * t_ref.shape[2]
    decay = d_ref[...]
    y, zh = lax.axis_index(Y), lax.axis_index(ZH)
    jump = jnp.exp(-decay * (zs * length))
    later = jnp.zeros_like(decay)
    here = jnp.zeros_like(decay)
    for k in range(n - 1, -1, -1):
        state = get_state(t_ref[n - 1 - k, zs * rows :, :])
        later = jnp.where(k > y, later * jump + state, later)
        here = jnp.where(k == y, state, here)
    for z in range(zs):
        total = t_ref[0, pl.ds(z * rows, rows), :].astype(f32)
        for k in range(1, n):
            total = total + t_ref[k, pl.ds(z * rows, rows), :].astype(f32)
        far = (zs - 1 + zh - z).astype(f32) * length
        near = jnp.maximum(zh - z - 1, 0).astype(f32) * length
        carry = jnp.exp(-decay * far) * later
        carry = jnp.where(zh > z, carry + jnp.exp(-decay * near) * here, carry)
        for h in range(2):
            slot = 2 * (zs - z) - 1 - h
            out_ref[slot, :SUB, :] = total[h * SUB : (h + 1) * SUB].astype(bf16)
            put_state(out_ref.at[slot, SUB:, :], carry)


def weight_rows(w_ref, core, block, count):
    blocks = w_ref.shape[0] // (2 * SUB * count)
    rows = []
    for b in range(blocks):
        start = 2 * SUB * (block * blocks + b) + SUB * core
        rows.append(w_ref[pl.ds(pl.multiple_of(start, SUB), SUB), :])
    return jnp.concatenate(rows, axis=0)


def mixed_kernel(p_ref, w_ref, own_ref, other_ref, total):
    tok = own_ref.shape[1]
    total[...] = lax.dot_general(
        weight_rows(w_ref, lax.axis_index(CORE), 0, 1),
        p_ref[...],
        (((0,), (0,)), ((), ())),
        preferred_element_type=f32,
    )
    core = lax.axis_index(CORE)
    own_ref[...] = total[:, pl.ds(pl.multiple_of(core * tok, tok), tok)]
    other_ref[...] = total[:, pl.ds(pl.multiple_of((1 - core) * tok, tok), tok)]


def halves(core, own_ref, other_ref, count):
    for h, ref in ((core, own_ref), (1 - core, other_ref)):
        for b in range(count):
            at = pl.ds(pl.multiple_of(2 * SUB * b + SUB * h, SUB), SUB)
            yield at, ref, pl.ds(SUB * b, SUB)


def finish_kernel(m_ref, mr_ref, own_ref, other_ref, mixed_ref, go_ref):
    mixed_ref[...] = (m_ref[...] + mr_ref[...]).T.astype(bf16)
    for at, ref, src in halves(lax.axis_index(CORE), own_ref, other_ref, own_ref.shape[0] // SUB):
        go_ref[at, :] = ref[src, :]


def last_kernel(scale, t_hbm, yo_hbm, yx_hbm, i_hbm, v_hbm, d_hbm, c_hbm, gi_ref, gv_ref, gw_ref, t_ref, yo_ref, yx_ref, i_ref, v_ref, d_ref, c_ref, bt, sems):
    pairs = ((t_hbm, t_ref), (yo_hbm, yo_ref), (yx_hbm, yx_ref), (i_hbm, i_ref), (v_hbm, v_ref))
    fetch(sems, *pairs, (d_hbm, d_ref), (c_hbm, c_ref))
    tok = yo_ref.shape[0]
    half = i_ref.shape[0] // 2
    core = lax.axis_index(CORE)
    later = (1 - core).astype(f32) * tok
    for h, y_ref in ((core, yo_ref), (1 - core, yx_ref)):
        state = get_state(t_ref[1 - h, SUB:, :])
        total = t_ref[1 - h, :SUB, :].astype(f32)
        for z in range(1, t_ref.shape[0] // 2):
            state = state + get_state(t_ref[2 * z + 1 - h, SUB:, :])
            total = total + t_ref[2 * z + 1 - h, :SUB, :].astype(f32)
        gw_ref[pl.ds(pl.multiple_of(SUB * h, SUB), SUB), :] = total * scale
        decay = d_ref[h]
        state = state * jnp.exp(-decay * later) * c_ref[h]
        heads(y_ref, bt, state, jnp.exp(-decay), True)
        back = bt[...].T[:half].astype(bf16).astype(f32)
        for b in range(half // SUB):
            at = pl.ds(pl.multiple_of(2 * SUB * b + SUB * h, SUB), SUB)
            part = back[SUB * b : SUB * (b + 1)]
            gi_ref[at, :] = (part * v_ref[at, :].astype(f32)).astype(bf16)
            gv_ref[at, :] = (part * i_ref[at, :].astype(f32)).astype(bf16)


def call(kernel, name, outs, args, scratch=(), cost=None, remote=0, limit=24):
    specs = [pl.BlockSpec(memory_space=pltpu.VMEM)] * (len(args) - remote)
    specs += [pl.BlockSpec(memory_space=pl.ANY)] * remote
    return pl.pallas_call(
        kernel,
        out_shape=tuple(jax.ShapeDtypeStruct(s, t) for s, t in outs),
        in_specs=specs,
        out_specs=tuple([pl.BlockSpec(memory_space=pltpu.VMEM)] * len(outs)),
        scratch_shapes=[pltpu.VMEM(s, t) for s, t in scratch]
        + ([pltpu.SemaphoreType.DMA((remote,))] if remote else []),
        compiler_params=None if limit is None else pltpu.CompilerParams(vmem_limit_bytes=limit * 2**20),
        cost_estimate=cost,
        name=name,
    )(*args)


LONG = pl.CostEstimate(flops=10**11, bytes_accessed=0, transcendentals=0)


def swap(x, axes):
    return lax.all_to_all(x, axes, 0, 0, tiled=True)


def swap_back(x, axes):
    order = [list(range(lax.axis_size(axes)))[::-1]]
    return lax.all_to_all(x, axes, 0, 0, axis_index_groups=order, tiled=True)


def spread(x, axis):
    n, rows, m = x.shape
    return swap(x.reshape(n * rows, m), axis)


def shift(x, axis, k):
    n = lax.axis_size(axis)
    return lax.ppermute(x, axis, [(i, (i + k) % n) for i in range(n)])


def other_core(x):
    return lax.ppermute(x, "core", [(0, 1), (1, 0)])


def shards(outer_gate, inner_gate, value_proj, residues, decays, out_weight, out_grad):
    chan, tok = outer_gate.shape
    half = chan // 2
    length = 2 * tok
    all_chan, cols = out_weight.shape
    modes = decays.shape[1]
    ny, nh, nx, nz = (lax.axis_size(axis) for axis in ("y", "zh", "x", "zl"))
    chips = ny * nh

    packed = ((tok + chan, cols), bf16)
    gate = ((chan, tok), bf16)
    own, other = call(
        pack_kernel,
        "pack",
        [packed] * 2,
        (inner_gate, value_proj, outer_gate, out_grad),
        scratch=[gate] * 3 + [((tok, cols), bf16)],
        remote=4,
        limit=None,
    )
    other = other_core(other)
    coef = residues * jnp.sqrt(-jnp.expm1(-2.0 * decays))
    small = ((modes, LANES), f32)
    pair = ((2, modes, LANES), f32)
    decay, coef, decay_both, coef_both = call(
        modes_kernel, "modes", [small, small, pair, pair], (decays.T, coef.T)
    )

    columns = ((length, LANES), f32)
    yf, states = call(
        scan_forward_kernel,
        "scan_forward",
        [columns, ((chips, modes, LANES), f32)],
        (decay, coef, own, other),
        scratch=[((half, tok), bf16)] * 2 + [columns],
        remote=2,
    )
    states = swap_back(states, ("y", "zh"))
    (got,) = call(
        both_kernel, "both", [((2, tok + chan, cols), bf16)], (own, other), remote=2
    )
    product, filtered = call(
        heads_forward_kernel,
        "heads_forward",
        [((nz, half, length), bf16), ((2, half, tok), bf16)],
        (states, decay, coef, yf, got),
        scratch=[columns],
    )

    parts = call(
        back_kernel, "back", [((all_chan // nx, tok), bf16)] * nx, (out_weight, out_grad)
    )
    product = spread(product, "zl")
    parts = [parts[0]] + [shift(part, "x", k) for k, part in enumerate(parts) if k]

    parts = call(split_kernel, "split", [gate] * nz, parts, cost=LONG)
    own, *parts, product = lax.optimization_barrier((*parts, product))
    own, other = call(
        sum_kernel,
        "sum",
        [((half, tok), f32)] * 2,
        (own, *(shift(part, "zl", k + 1) for k, part in enumerate(parts))),
    )
    product = spread(jnp.broadcast_to(product[None], (nx,) + product.shape), "x")
    half_columns = ((tok, LANES), f32)
    yb, yb_other, state, grad_outer, grad_outer_other = call(
        scan_backward_kernel,
        "scan_backward",
        [half_columns] * 2 + [((modes, 2 * LANES), bf16)] + [((half, tok), bf16)] * 2,
        (own, other_core(other), filtered, got, decay, coef),
        scratch=[columns] * 2,
    )

    (partial,) = call(
        weight_kernel,
        "weight",
        [((ny, nh * 2 * SUB + modes, cols), bf16)],
        (product, got, state),
    )
    partial = swap_back(partial, "y")
    last = ((2 * nh, SUB + modes, cols), bf16)
    (partial,) = call(middle_kernel, "middle", [last], (partial, decay))
    partial = swap_back(partial, ("zh", "core"))
    mixed, mixed_other = call(
        mixed_kernel,
        "mixed",
        [((cols, tok), f32)] * 2,
        (product, out_weight),
        scratch=[((cols, length), f32)],
    )
    mixed, grad_outer = call(
        finish_kernel,
        "finish",
        [((tok, cols), bf16), gate],
        (mixed, other_core(mixed_other), grad_outer, other_core(grad_outer_other)),
    )
    mixed, grad_outer, partial = lax.optimization_barrier((mixed, grad_outer, partial))
    scale = 1.0 / math.sqrt(length * chips)
    grad_inner, grad_value, grad_weight = call(
        lambda *refs: last_kernel(scale, *refs),
        "last",
        [gate, gate, ((2 * SUB, cols), f32)],
        (
            partial.reshape(last[0]),
            yb,
            other_core(yb_other),
            inner_gate,
            value_proj,
            decay_both,
            coef_both,
        ),
        scratch=[last, half_columns, half_columns, gate, gate, pair, pair, half_columns],
        remote=7,
        limit=None,
    )
    return (mixed, grad_outer, grad_inner, grad_value, grad_weight)


def solution(mesh):
    fine = Mesh(mesh.devices.reshape(8, 3, 2, 4, 4), ("y", "zh", "core", "x", "zl"))
    seq, col = ("y", "zh", "core"), ("x", "zl")
    return jax.shard_map(
        shards,
        mesh=fine,
        in_specs=(
            P(col, seq),
            P(col, seq),
            P(col, seq),
            P(col, None),
            P(col, None),
            P(None, col),
            P(seq, col),
        ),
        out_specs=(P(seq, col), P(col, seq), P(col, seq), P(col, seq), P(seq, col)),
        check_vma=False,
    )
```

```python
import math

import jax
import jax.numpy as jnp
from jax import lax
from jax.experimental import pallas as pl
from jax.experimental.pallas import tpu as pltpu
from jax.sharding import Mesh
from jax.sharding import PartitionSpec as P

f32 = jnp.float32
bf16 = jnp.bfloat16
SUB = 32
LANES = 128
CORE, X, ZL, Y, ZH, CHIP = "core", "x", "zl", "y", "zh", ("y", "zh")


def to_columns(tile):
    rows, width = tile.shape
    pad = jnp.zeros((LANES - rows, width), f32)
    return jnp.concatenate([tile, pad], axis=0).T


def pack_kernel(i_hbm, v_hbm, o_hbm, g_hbm, own_ref, other_ref, i_ref, v_ref, o_ref, g_ref, sems):
    fetch(sems, (i_hbm, i_ref), (v_hbm, v_ref), (o_hbm, o_ref), (g_hbm, g_ref))
    tok = g_ref.shape[0]
    half = i_ref.shape[0] // 2
    core = lax.axis_index(CORE)
    for h, ref in ((core, own_ref), (1 - core, other_ref)):
        ref[:tok] = g_ref[...]
        for b in range(half // SUB):
            src = pl.ds(pl.multiple_of(2 * SUB * b + SUB * h, SUB), SUB)
            gated = (i_ref[src, :].astype(f32) * v_ref[src, :].astype(f32)).astype(bf16)
            ref[pl.ds(tok + SUB * b, SUB), :] = gated
            ref[pl.ds(tok + half + SUB * b, SUB), :] = o_ref[src, :]


def fetch(sems, *pairs):
    copies = [pltpu.make_async_copy(src, dst, sems.at[k]) for k, (src, dst) in enumerate(pairs)]
    for copy in copies:
        copy.start()
    for copy in copies:
        copy.wait()


def both_kernel(own_hbm, other_hbm, out_ref, sems):
    core = lax.axis_index(CORE)
    fetch(sems, (own_hbm, out_ref.at[core]), (other_hbm, out_ref.at[1 - core]))


def modes_kernel(d_ref, c_ref, od_ref, oc_ref, ad_ref, ac_ref):
    chan = lax.broadcasted_iota(jnp.int32, (d_ref.shape[1], LANES), 0)
    lane = lax.broadcasted_iota(jnp.int32, (d_ref.shape[1], LANES), 1)
    for src, own, both in ((d_ref, od_ref, ad_ref), (c_ref, oc_ref, ac_ref)):
        for h in range(2):
            wanted = lane + SUB * (lane // SUB) + SUB * h
            pick = jnp.where((chan == wanted) & (lane < d_ref.shape[1] // 2), 1.0, 0.0)
            both[h] = jnp.dot(
                src[...],
                pick.astype(f32),
                precision=lax.Precision.HIGHEST,
                preferred_element_type=f32,
            )
        own[...] = both[lax.axis_index(CORE)]


def back_kernel(w_ref, g_ref, *outs):
    chan = 6 * SUB
    n = len(outs)
    rows = w_ref.shape[0] // n
    grads = g_ref[...]
    for k, ref in enumerate(outs):
        block = lax.rem(lax.axis_index(X) + k, n)
        for j in range(rows // chan):
            at = pl.ds(pl.multiple_of(block * rows + j * chan, chan), chan)
            part = lax.dot_general(
                w_ref[at, :], grads, (((1,), (1,)), ((), ())), preferred_element_type=f32
            ).astype(bf16)
            for b in range(6):
                dst = j * chan + (b % 2) * 3 * SUB + (b // 2) * SUB
                ref[pl.ds(dst, SUB), :] = part[b * SUB : (b + 1) * SUB]


def split_kernel(p0, p1, p2, p3, *outs):
    rows = p0.shape[0] // len(outs)
    for k, ref in enumerate(outs):
        block = lax.rem(lax.axis_index(ZL) + k, len(outs))
        at = pl.ds(pl.multiple_of(block * rows, rows), rows)
        total = p0[at, :].astype(f32)
        for p in (p1, p2, p3):
            total = total + p[at, :].astype(f32)
        ref[...] = total.astype(bf16)


def sum_kernel(p0, p1, p2, p3, own_ref, other_ref):
    half = own_ref.shape[0]
    core = lax.axis_index(CORE)
    for h, ref in ((core, own_ref), (1 - core, other_ref)):
        at = pl.ds(pl.multiple_of(h * half, half), half)
        total = p0[at, :].astype(f32)
        for p in (p1, p2, p3):
            total = total + p[at, :].astype(f32)
        ref[...] = total


def scan(src, y_ref, rate, coef, reverse):
    length = src.shape[0]

    def step(i, state):
        lo = length - 8 - i * 8 if reverse else i * 8
        at = pl.ds(pl.multiple_of(lo, 8), 8)
        block = src[at, :]
        rows = [None] * 8
        for t in range(8):
            u = 7 - t if reverse else t
            state = state * rate + block[u : u + 1, :]
            rows[u] = jnp.sum(state * coef, axis=0, keepdims=True)
        y_ref[at, :] = jnp.concatenate(rows, axis=0)
        return state

    return lax.fori_loop(0, length // 8, step, jnp.zeros_like(coef))


def heads(y_ref, out, state, rate, reverse):
    length = y_ref.shape[0]

    def step(i, state):
        lo = length - 8 - i * 8 if reverse else i * 8
        at = pl.ds(pl.multiple_of(lo, 8), 8)
        rows = [None] * 8
        for t in range(8):
            u = 7 - t if reverse else t
            state = state * rate
            rows[u] = jnp.sum(state, axis=0, keepdims=True)
        out[at, :] = y_ref[at, :] + jnp.concatenate(rows, axis=0)
        return state

    lax.fori_loop(0, length // 8, step, state)


def scan_forward_kernel(d_ref, c_ref, own_hbm, other_hbm, y_ref, s_ref, own_ref, other_ref, gt, sems):
    half, tok = own_ref.shape
    gated = pl.ds(tok, half)
    fetch(sems, (own_hbm.at[gated], own_ref), (other_hbm.at[gated], other_ref))
    core = lax.axis_index(CORE)
    for h, ref in ((core, own_ref), (1 - core, other_ref)):
        at = pl.ds(pl.multiple_of(h * tok, tok), tok)
        gt[at, :] = to_columns(ref[...].astype(f32))
    state = scan(gt, y_ref, jnp.exp(-d_ref[...]), c_ref[...], False)
    for m in range(s_ref.shape[0]):
        s_ref[m] = state


def heads_forward_kernel(s_ref, d_ref, c_ref, y_ref, got_ref, p_ref, f_ref, ft):
    tok = got_ref.shape[2]
    half = f_ref.shape[1]
    decay = d_ref[...]
    jump = jnp.exp(-decay * float(ft.shape[0]))
    state = jnp.zeros_like(decay)
    chips = s_ref.shape[0]
    for m in range(chips):
        state = jnp.where(m < lax.axis_index(CHIP), state * jump + s_ref[chips - 1 - m], state)
    heads(y_ref, ft, state * c_ref[...], jnp.exp(-decay), False)
    for h in range(2):
        at = pl.ds(h * tok, tok)
        filtered = ft[at, :].T[:half].astype(bf16)
        f_ref[h] = filtered
        product = (got_ref[h, tok + half :].astype(f32) * filtered.astype(f32)).astype(bf16)
        for q in range(p_ref.shape[0]):
            p_ref[q, :, at] = product


def scan_backward_kernel(own_ref, other_ref, f_ref, got_ref, d_ref, c_ref, yo_ref, x_ref, s_ref, go_ref, bt, y_ref):
    tok = got_ref.shape[2]
    half = own_ref.shape[0]
    core = lax.axis_index(CORE)
    for h, ref in ((core, own_ref), (1 - core, other_ref)):
        total = ref[...]
        grad_outer = (total * f_ref[h].astype(f32)).astype(bf16)
        if ref is own_ref:
            go_ref[...] = grad_outer
        else:
            x_ref[:, LANES:] = to_columns(grad_outer.astype(f32))
        outer = got_ref[h, tok + half :].astype(f32)
        at = pl.ds(pl.multiple_of(h * tok, tok), tok)
        bt[at, :] = to_columns((total * outer).astype(bf16).astype(f32))
    state = scan(bt, y_ref, jnp.exp(-d_ref[...]), c_ref[...], True)
    put_state(s_ref, state)
    yo_ref[...] = y_ref[pl.ds(pl.multiple_of(core * tok, tok), tok), :]
    x_ref[:, :LANES] = y_ref[pl.ds(pl.multiple_of((1 - core) * tok, tok), tok), :]


def put_state(ref, state):
    first = state.astype(bf16)
    ref[:, :LANES] = first
    ref[:, LANES:] = (state - first.astype(f32)).astype(bf16)


def get_state(ref):
    both = ref.astype(f32)
    return both[:, :LANES] + both[:, LANES:]


def weight_kernel(p_ref, got_ref, s_ref, out_ref):
    tok = got_ref.shape[2]
    n = out_ref.shape[0]
    rows = p_ref.shape[0] // n
    grads = got_ref[:, :tok, :].reshape(2 * tok, -1)
    for y in range(n):
        part = jnp.dot(p_ref[pl.ds(y * rows, rows), :], grads, preferred_element_type=f32)
        out_ref[n - 1 - y, :rows, :] = part.astype(bf16)
        out_ref[n - 1 - y, rows:, :] = s_ref[...]


def middle_kernel(t_ref, d_ref, out_ref):
    n = t_ref.shape[0]
    zs, rows = out_ref.shape[0] // 2, 2 * SUB
    length = 2.0 * t_ref.shape[2]
    decay = d_ref[...]
    y, zh = lax.axis_index(Y), lax.axis_index(ZH)
    jump = jnp.exp(-decay * (zs * length))
    later = jnp.zeros_like(decay)
    here = jnp.zeros_like(decay)
    for k in range(n - 1, -1, -1):
        state = get_state(t_ref[n - 1 - k, zs * rows :, :])
        later = jnp.where(k > y, later * jump + state, later)
        here = jnp.where(k == y, state, here)
    for z in range(zs):
        total = t_ref[0, pl.ds(z * rows, rows), :].astype(f32)
        for k in range(1, n):
            total = total + t_ref[k, pl.ds(z * rows, rows), :].astype(f32)
        far = (zs - 1 + zh - z).astype(f32) * length
        near = jnp.maximum(zh - z - 1, 0).astype(f32) * length
        carry = jnp.exp(-decay * far) * later
        carry = jnp.where(zh > z, carry + jnp.exp(-decay * near) * here, carry)
        for h in range(2):
            slot = 2 * (zs - z) - 1 - h
            out_ref[slot, :SUB, :] = total[h * SUB : (h + 1) * SUB].astype(bf16)
            put_state(out_ref.at[slot, SUB:, :], carry)


def weight_rows(w_ref, core, block, count):
    blocks = w_ref.shape[0] // (2 * SUB * count)
    rows = []
    for b in range(blocks):
        start = 2 * SUB * (block * blocks + b) + SUB * core
        rows.append(w_ref[pl.ds(pl.multiple_of(start, SUB), SUB), :])
    return jnp.concatenate(rows, axis=0)


def mixed_kernel(p_ref, w_ref, own_ref, other_ref, total):
    tok = own_ref.shape[1]
    total[...] = lax.dot_general(
        weight_rows(w_ref, lax.axis_index(CORE), 0, 1),
        p_ref[...],
        (((0,), (0,)), ((), ())),
        preferred_element_type=f32,
    )
    core = lax.axis_index(CORE)
    own_ref[...] = total[:, pl.ds(pl.multiple_of(core * tok, tok), tok)]
    other_ref[...] = total[:, pl.ds(pl.multiple_of((1 - core) * tok, tok), tok)]


def finish_kernel(m_ref, mr_ref, own_ref, x_ref, mixed_ref, go_ref):
    mixed_ref[...] = (m_ref[...] + mr_ref[...]).T.astype(bf16)
    half = own_ref.shape[0]
    other = x_ref[:, LANES:].T[:half].astype(bf16)
    core = lax.axis_index(CORE)
    for h, part in ((core, own_ref[...]), (1 - core, other)):
        for b in range(half // SUB):
            at = pl.ds(pl.multiple_of(2 * SUB * b + SUB * h, SUB), SUB)
            go_ref[at, :] = part[SUB * b : SUB * (b + 1)]


def last_kernel(scale, t_hbm, yo_hbm, x_hbm, i_hbm, v_hbm, d_hbm, c_hbm, gi_ref, gv_ref, gw_ref, t_ref, yo_ref, yx_ref, i_ref, v_ref, d_ref, c_ref, bt, sems):
    part = x_hbm.at[:, pl.ds(0, LANES)]
    pairs = ((t_hbm, t_ref), (yo_hbm, yo_ref), (part, yx_ref), (i_hbm, i_ref), (v_hbm, v_ref))
    fetch(sems, *pairs, (d_hbm, d_ref), (c_hbm, c_ref))
    tok = yo_ref.shape[0]
    half = i_ref.shape[0] // 2
    core = lax.axis_index(CORE)
    later = (1 - core).astype(f32) * tok
    for h, y_ref in ((core, yo_ref), (1 - core, yx_ref)):
        state = get_state(t_ref[1 - h, SUB:, :])
        total = t_ref[1 - h, :SUB, :].astype(f32)
        for z in range(1, t_ref.shape[0] // 2):
            state = state + get_state(t_ref[2 * z + 1 - h, SUB:, :])
            total = total + t_ref[2 * z + 1 - h, :SUB, :].astype(f32)
        gw_ref[pl.ds(pl.multiple_of(SUB * h, SUB), SUB), :] = total * scale
        decay = d_ref[h]
        state = state * jnp.exp(-decay * later) * c_ref[h]
        heads(y_ref, bt, state, jnp.exp(-decay), True)
        back = bt[...].T[:half].astype(bf16).astype(f32)
        for b in range(half // SUB):
            at = pl.ds(pl.multiple_of(2 * SUB * b + SUB * h, SUB), SUB)
            part = back[SUB * b : SUB * (b + 1)]
            gi_ref[at, :] = (part * v_ref[at, :].astype(f32)).astype(bf16)
            gv_ref[at, :] = (part * i_ref[at, :].astype(f32)).astype(bf16)


def call(kernel, name, outs, args, scratch=(), cost=None, remote=0, limit=24):
    specs = [pl.BlockSpec(memory_space=pltpu.VMEM)] * (len(args) - remote)
    specs += [pl.BlockSpec(memory_space=pl.ANY)] * remote
    return pl.pallas_call(
        kernel,
        out_shape=tuple(jax.ShapeDtypeStruct(s, t) for s, t in outs),
        in_specs=specs,
        out_specs=tuple([pl.BlockSpec(memory_space=pltpu.VMEM)] * len(outs)),
        scratch_shapes=[pltpu.VMEM(s, t) for s, t in scratch]
        + ([pltpu.SemaphoreType.DMA((remote,))] if remote else []),
        compiler_params=None if limit is None else pltpu.CompilerParams(vmem_limit_bytes=limit * 2**20),
        cost_estimate=cost,
        name=name,
    )(*args)


LONG = pl.CostEstimate(flops=10**11, bytes_accessed=0, transcendentals=0)


def swap(x, axes):
    return lax.all_to_all(x, axes, 0, 0, tiled=True)


def swap_back(x, axes):
    order = [list(range(lax.axis_size(axes)))[::-1]]
    return lax.all_to_all(x, axes, 0, 0, axis_index_groups=order, tiled=True)


def spread(x, axis):
    n, rows, m = x.shape
    return swap(x.reshape(n * rows, m), axis)


def shift(x, axis, k):
    n = lax.axis_size(axis)
    return lax.ppermute(x, axis, [(i, (i + k) % n) for i in range(n)])


def other_core(x):
    return lax.ppermute(x, "core", [(0, 1), (1, 0)])


def shards(outer_gate, inner_gate, value_proj, residues, decays, out_weight, out_grad):
    chan, tok = outer_gate.shape
    half = chan // 2
    length = 2 * tok
    all_chan, cols = out_weight.shape
    modes = decays.shape[1]
    ny, nh, nx, nz = (lax.axis_size(axis) for axis in ("y", "zh", "x", "zl"))
    chips = ny * nh

    packed = ((tok + chan, cols), bf16)
    gate = ((chan, tok), bf16)
    own, other = call(
        pack_kernel,
        "pack",
        [packed] * 2,
        (inner_gate, value_proj, outer_gate, out_grad),
        scratch=[gate] * 3 + [((tok, cols), bf16)],
        remote=4,
        limit=None,
    )
    other = other_core(other)
    coef = residues * jnp.sqrt(-jnp.expm1(-2.0 * decays))
    small = ((modes, LANES), f32)
    pair = ((2, modes, LANES), f32)
    decay, coef, decay_both, coef_both = call(
        modes_kernel, "modes", [small, small, pair, pair], (decays.T, coef.T)
    )

    columns = ((length, LANES), f32)
    yf, states = call(
        scan_forward_kernel,
        "scan_forward",
        [columns, ((chips, modes, LANES), f32)],
        (decay, coef, own, other),
        scratch=[((half, tok), bf16)] * 2 + [columns],
        remote=2,
    )
    states = swap_back(states, ("y", "zh"))
    (got,) = call(
        both_kernel, "both", [((2, tok + chan, cols), bf16)], (own, other), remote=2
    )
    product, filtered = call(
        heads_forward_kernel,
        "heads_forward",
        [((nz, half, length), bf16), ((2, half, tok), bf16)],
        (states, decay, coef, yf, got),
        scratch=[columns],
    )

    parts = call(
        back_kernel, "back", [((all_chan // nx, tok), bf16)] * nx, (out_weight, out_grad)
    )
    product = spread(product, "zl")
    parts = [parts[0]] + [shift(part, "x", k) for k, part in enumerate(parts) if k]

    parts = call(split_kernel, "split", [gate] * nz, parts, cost=LONG)
    own, *parts, product = lax.optimization_barrier((*parts, product))
    own, other = call(
        sum_kernel,
        "sum",
        [((half, tok), f32)] * 2,
        (own, *(shift(part, "zl", k + 1) for k, part in enumerate(parts))),
    )
    product = spread(jnp.broadcast_to(product[None], (nx,) + product.shape), "x")
    half_columns = ((tok, LANES), f32)
    yb, other, state, grad_outer = call(
        scan_backward_kernel,
        "scan_backward",
        [half_columns, ((tok, 2 * LANES), f32), ((modes, 2 * LANES), bf16), ((half, tok), bf16)],
        (own, other_core(other), filtered, got, decay, coef),
        scratch=[columns] * 2,
    )

    (partial,) = call(
        weight_kernel,
        "weight",
        [((ny, nh * 2 * SUB + modes, cols), bf16)],
        (product, got, state),
    )
    partial = swap_back(partial, "y")
    last = ((2 * nh, SUB + modes, cols), bf16)
    (partial,) = call(middle_kernel, "middle", [last], (partial, decay))
    partial = swap_back(partial, ("zh", "core"))
    other = other_core(other)
    mixed, mixed_other = call(
        mixed_kernel,
        "mixed",
        [((cols, tok), f32)] * 2,
        (product, out_weight),
        scratch=[((cols, length), f32)],
    )
    mixed, grad_outer = call(
        finish_kernel,
        "finish",
        [((tok, cols), bf16), gate],
        (mixed, other_core(mixed_other), grad_outer, other),
    )
    mixed, grad_outer, partial = lax.optimization_barrier((mixed, grad_outer, partial))
    scale = 1.0 / math.sqrt(length * chips)
    grad_inner, grad_value, grad_weight = call(
        lambda *refs: last_kernel(scale, *refs),
        "last",
        [gate, gate, ((2 * SUB, cols), f32)],
        (
            partial.reshape(last[0]),
            yb,
            other,
            inner_gate,
            value_proj,
            decay_both,
            coef_both,
        ),
        scratch=[last, half_columns, half_columns, gate, gate, pair, pair, half_columns],
        remote=7,
        limit=None,
    )
    return (mixed, grad_outer, grad_inner, grad_value, grad_weight)


def solution(mesh):
    fine = Mesh(mesh.devices.reshape(8, 3, 2, 4, 4), ("y", "zh", "core", "x", "zl"))
    seq, col = ("y", "zh", "core"), ("x", "zl")
    return jax.shard_map(
        shards,
        mesh=fine,
        in_specs=(
            P(col, seq),
            P(col, seq),
            P(col, seq),
            P(col, None),
            P(col, None),
            P(None, col),
            P(seq, col),
        ),
        out_specs=(P(seq, col), P(col, seq), P(col, seq), P(col, seq), P(seq, col)),
        check_vma=False,
    )
```
